32 devices in a mesh: gx: 4 (over y, x), gy: 4 (over z), gz: 2 (over core).
Axes of the slice: x: 2, y: 2, z: 4, core: 2. Of those that a mesh axis runs over, the one named last changes fastest.
Arguments:
- boxes: bfloat16 [4, 4, 2, 16, 16, 256], P('gx', 'gy', 'gz'), may hold values from 0 to 2
- anchors: int32 [4, 4, 2, 16, 3], P('gx', 'gy', 'gz'), may hold values from 0 to 4, as said below
- potential: float32 [160, 160, 80], P('gx', 'gy', 'gz'), may hold values from 0.5 to 2
Outputs:
- relaxed: bfloat16 [4, 4, 2, 16, 16, 256], P('gx', 'gy', 'gz')
The draws below stay inside these ranges and needn't reach their ends.
Inputs may be any that keep to these rules, and one draw needn't show every extreme that they name: `anchors`: in every region exactly 8 of the 16 functions are border functions, and every coordinate of theirs is 0 or 4; all coordinates of the others lie within 1 to 3.
All inputs are finite; a program needn't handle non-finite values.
Results may differ from the reference program's by a relative error of at most 0.0041.
Values may be sent and summed in bfloat16 or wider, within the bound.
A program may use at most 128 MiB of HBM per device.

```python
import math
import jax
import jax.numpy as jnp
from jax import lax

FUNCS = 16
EXPORT = 8
REGION = 5
BOX = 16
SWEEPS = 2
RCELLS = 40
GRIDX = 4
GRIDY = 4
GRIDZ = 2
CELLSX = 160
CELLSY = 160
CELLSZ = 80


def draw_anchors(key, part):
    key_inside, key_value, key_order = jax.random.split(key, 3)
    grid_shape = (GRIDX, GRIDY, GRIDZ, FUNCS)
    inside_pos = jax.random.randint(key_inside, grid_shape + (3,), 1, REGION - 1)
    touching_pos = jax.random.randint(key_value, grid_shape + (3,), 0, 2) * (REGION - 1)
    scores = jax.random.randint(key_order, grid_shape, 0, 1 << 20) * FUNCS + jnp.arange(FUNCS, dtype=jnp.int32)
    ranking = jnp.argsort(jnp.argsort(scores, axis=-1, stable=True), axis=-1, stable=True)
    return jnp.where((ranking < EXPORT)[..., None], touching_pos, inside_pos).astype(jnp.int32)


def block_scale(key, dims, pieces, low, top_value):
    gain = 1.0
    for dim, shards_of in pieces:
        draws = jax.random.uniform(jax.random.fold_in(jax.random.fold_in(key, 6), dim), (shards_of,), jnp.float32, low / len(pieces), top_value / len(pieces))
        gain = gain * jnp.repeat(jnp.exp(draws), dims[dim] // shards_of).reshape((-1,) + (1,) * (len(dims) - 1 - dim))
    return gain


def setup_inputs(seed: int = 0) -> dict:
    key_list = jax.random.split(jax.random.key(seed), 4)
    return {
        "boxes": jnp.clip(2.0 * jax.random.uniform(key_list[0], (GRIDX, GRIDY, GRIDZ, FUNCS, BOX, BOX * BOX), jnp.float32) ** block_scale(key_list[0], (GRIDX, GRIDY, GRIDZ, FUNCS, BOX, BOX * BOX), ((0, 4), (1, 4), (2, 2)), -0.2, 0.2), 0.0, 2.0).astype(jnp.bfloat16),
        "anchors": draw_anchors(jax.random.fold_in(key_list[3], 71), 0),
        "potential": jnp.clip(jnp.exp(math.log(2.0) - 1.3862944 * jax.random.uniform(key_list[2], (CELLSX, CELLSY, CELLSZ), jnp.float32) ** block_scale(key_list[2], (CELLSX, CELLSY, CELLSZ), ((0, 4), (1, 4), (2, 2)), -0.2, 0.2)), 0.5, 2.0),
    }


MAGIC = [8.4334247333529341e-7, -1.2905572013420610e-5, 8.7629844762105596e-5, -3.0158038132690463e-4, 1.7472371367299390e-3, -9.4204703020108039e-3, 2.3738214637249424e-2, 6.1262589583120798e-2, 0.9940415697834004, -6.0489528919698352e-2, -2.1030251609303814e-2, 1.3372634148547948e-2, -3.4412814449349386e-3, 4.9443227688689919e-4, -5.1859868811734329e-5, 2.7273449291197966e-6]
KINETIC = [-3.5536922899131902, 2.2191465938911164, -0.6156141465570069, 0.2371780582153806, -0.0822663999742123, 0.0220702918848226, -4.0976568934263382e-3, 4.5167920287502235e-4, -2.3982285245075997e-5, 2.0904234952920366e-6, -3.7230763047369276e-7, -1.0585705549674147e-8, -5.8138798302825405e-11, 2.7080049362631944e-13, -6.9244749406392002e-18]
CELL = 1.0 / 4096.0
STEP = 0.1
PENALTY = 3.0


def magic_table(amount):
    row_ids = jnp.arange(amount)[:, None]
    col_ids = jnp.arange(amount)[None, :]
    offset = col_ids - row_ids + 8
    coeffs = jnp.array(MAGIC, dtype=jnp.float32)
    picked = coeffs[jnp.clip(offset, 0, 15)]
    return jnp.where((offset >= 0) & (offset < 16), picked, jnp.zeros_like(picked))


def kinetic_table(amount):
    row_ids = jnp.arange(amount)[:, None]
    col_ids = jnp.arange(amount)[None, :]
    distance = jnp.abs(col_ids - row_ids)
    coeffs = jnp.array(KINETIC, dtype=jnp.float32)
    picked = coeffs[jnp.clip(distance, 0, 14)]
    return jnp.where(distance < 15, picked, jnp.zeros_like(picked))


def apply_hamiltonian(values, potential_box):
    highest = lax.Precision.HIGHEST
    amount = values.shape[1]
    magic = magic_table(amount)
    second = kinetic_table(amount)
    identity_small = jnp.eye(amount, dtype=jnp.float32)
    magic_pair = jnp.kron(magic, magic)
    second_pair = jnp.kron(second, identity_small) + jnp.kron(identity_small, second)
    on_grid = jnp.einsum("xw,fwc->fxc", magic, values, precision=highest)
    on_grid = jnp.einsum("dc,fxc->fxd", magic_pair, on_grid, precision=highest)
    weighted = potential_box * on_grid
    returned = jnp.einsum("wx,fwc->fxc", magic, weighted, precision=highest)
    returned = jnp.einsum("cd,fxc->fxd", magic_pair, returned, precision=highest)
    kinetic = jnp.einsum("xw,fwc->fxc", second, values, precision=highest)
    kinetic = kinetic + jnp.einsum("dc,fxc->fxd", second_pair, values, precision=highest)
    return returned - 0.5 * kinetic


def border_rows(anchor_rows):
    amount = anchor_rows.shape[0]
    touching = jnp.any((anchor_rows == 0) | (anchor_rows == REGION - 1), axis=1).astype(jnp.int32)
    ranking = jnp.cumsum(touching) - touching
    places = jnp.arange(EXPORT, dtype=jnp.int32)
    matched = (touching[None, :] == 1) & (ranking[None, :] == places[:, None])
    numbers = jnp.arange(amount, dtype=jnp.int32)[None, :]
    return jnp.sum(jnp.where(matched, numbers, 0), axis=1).astype(jnp.int32)


def octants(values):
    amount = values.shape[0]
    half_width = values.shape[1] // 2
    split_up = values.reshape(amount, 2, half_width, 2, half_width, 2, half_width)
    return split_up.transpose(0, 1, 3, 5, 2, 4, 6).reshape(amount * 8, half_width ** 3)


def from_octants(values, amount, width):
    half_width = width // 2
    split_up = values.reshape(amount, 2, 2, 2, half_width, half_width, half_width)
    return split_up.transpose(0, 1, 4, 2, 5, 3, 6).reshape(amount, width, width * width)


def octant_mask(left_anchor, right_anchor):
    labels = jnp.arange(8, dtype=jnp.int32)
    corner_bits = jnp.stack([labels // 4, (labels // 2) % 2, labels % 2], axis=1)
    left_place = left_anchor[:, None, :] + corner_bits[None]
    right_place = right_anchor[:, None, :] + corner_bits[None]
    result = jnp.ones((left_anchor.shape[0], 8, right_anchor.shape[0], 8), jnp.float32)
    for dimension in range(3):
        equal = left_place[:, :, None, None, dimension] == right_place[None, None, :, :, dimension]
        result = result * equal.astype(jnp.float32)
    return result


def combine(current, own_anchor, applied, cand_boxes, cand_anchor):
    func_count = current.shape[0]
    cand_count = cand_boxes.shape[0]
    width = current.shape[1]
    stacked = octants(jnp.concatenate([current, applied.astype(jnp.bfloat16)], axis=0))
    columns = octants(cand_boxes)
    products = jnp.einsum("ak,bk->ab", stacked.astype(jnp.float32), columns.astype(jnp.float32), precision=lax.Precision.HIGHEST)
    products = products.reshape(2, func_count, 8, cand_count, 8)
    geometry = octant_mask(own_anchor, cand_anchor)
    intersection = CELL * jnp.sum(products * geometry[None], axis=(2, 4))
    identity = (jnp.arange(func_count)[:, None] == jnp.arange(cand_count)[None, :]).astype(jnp.float32)
    coupling = intersection[1] - PENALTY * (intersection[0] - identity)
    weights = (coupling[:, None, :, None] * geometry).astype(jnp.bfloat16).reshape(func_count * 8, cand_count * 8)
    correction = jnp.dot(weights, columns, preferred_element_type=jnp.float32)
    correction = from_octants(correction, func_count, width)
    return (current.astype(jnp.float32) - STEP * (applied - correction)).astype(jnp.bfloat16)


def reference(boxes, anchors, potential):
    width = boxes.shape[4]
    half_width = width // 2
    func_count = boxes.shape[3]
    region_count = GRIDX * GRIDY * GRIDZ
    padded = jnp.concatenate([potential, potential[:half_width]], axis=0)
    padded = jnp.concatenate([padded, padded[:, :half_width]], axis=1)
    padded = jnp.concatenate([padded, padded[:, :, :half_width]], axis=2)
    flat_anchor = anchors.reshape(region_count, func_count, 3)
    chosen_all = jax.vmap(border_rows)(flat_anchor)
    exported_anchor = jnp.take_along_axis(flat_anchor, chosen_all[:, :, None], axis=1).reshape(GRIDX, GRIDY, GRIDZ, EXPORT, 3)
    current_all = boxes
    for sweep_index in range(SWEEPS):
        exported = jnp.take_along_axis(current_all.reshape(region_count, func_count, width, width * width), chosen_all[:, :, None, None], axis=1)
        exported = exported.reshape(GRIDX, GRIDY, GRIDZ, EXPORT, width, width * width)
        previous = current_all

        def one_region(region):
            place_x = region // (GRIDY * GRIDZ)
            place_y = (region // GRIDZ) % GRIDY
            place_z = region % GRIDZ
            current = previous[place_x, place_y, place_z]
            own_anchor = anchors[place_x, place_y, place_z]
            corner = jnp.stack([place_x, place_y, place_z]).astype(jnp.int32) * RCELLS

            def cut_box(anchor_row):
                start = corner + half_width * anchor_row
                return lax.dynamic_slice(padded, (start[0], start[1], start[2]), (width, width, width))

            potential_box = jax.vmap(cut_box)(own_anchor).reshape(func_count, width, width * width)
            applied = apply_hamiltonian(current.astype(jnp.float32), potential_box)
            piece_boxes = [current]
            piece_anchor = [own_anchor]
            for step_x in (-1, 0, 1):
                for step_y in (-1, 0, 1):
                    for step_z in (-1, 0, 1):
                        if (step_x, step_y, step_z) != (0, 0, 0):
                            near_x = (place_x + step_x) % GRIDX
                            near_y = (place_y + step_y) % GRIDY
                            near_z = (place_z + step_z) % GRIDZ
                            piece_boxes.append(exported[near_x, near_y, near_z])
                            moved = REGION * jnp.array([step_x, step_y, step_z], dtype=jnp.int32)
                            piece_anchor.append(exported_anchor[near_x, near_y, near_z] + moved[None, :])
            cand_boxes = jnp.concatenate(piece_boxes, axis=0)
            cand_anchor = jnp.concatenate(piece_anchor, axis=0)
            return combine(current, own_anchor, applied, cand_boxes, cand_anchor)

        current_all = lax.map(one_region, jnp.arange(region_count, dtype=jnp.int32)).reshape(boxes.shape)
    return current_all
```

```python
import functools

import jax
import jax.numpy as jnp
import ml_dtypes
import numpy as np
from jax import lax
from jax.experimental import pallas as pl
from jax.experimental.pallas import tpu as pltpu
from jax.sharding import PartitionSpec as P

REGION = 5
SWEEPS = 2
MAGIC = [
    8.433424733352934e-07,
    -1.290557201342061e-05,
    8.76298447621056e-05,
    -0.00030158038132690465,
    0.001747237136729939,
    -0.009420470302010804,
    0.023738214637249424,
    0.0612625895831208,
    0.9940415697834004,
    -0.06048952891969835,
    -0.021030251609303816,
    0.013372634148547948,
    -0.0034412814449349387,
    0.0004944322768868992,
    -5.185986881173433e-05,
    2.7273449291197967e-06,
]
KINETIC = [
    -3.55369228991319,
    2.2191465938911166,
    -0.6156141465570069,
    0.2371780582153806,
    -0.0822663999742123,
    0.0220702918848226,
    -0.004097656893426338,
    0.00045167920287502236,
    -2.3982285245075998e-05,
    2.0904234952920368e-06,
    -3.7230763047369276e-07,
    -1.0585705549674146e-08,
    -5.8138798302825403e-11,
    2.7080049362631943e-13,
    -6.9244749406392e-18,
]
CELL = 1.0 / 4096.0
STEP = 0.1
PENALTY = 3.0
BF = jnp.bfloat16
F32 = jnp.float32
MESH = pl.DeviceIdType.MESH
AXES = ("gx", "gy", "gz")

PCOL, PCOLT, PROW, RM, RK, RMT, LM, LMT, LK = 0, 1, 2, 3, 5, 7, 9, 11, 13


def make_tables():
    magic = np.zeros((16, 16))
    kinetic = np.zeros((16, 16))
    for r in range(16):
        for c in range(16):
            if -8 <= c - r <= 7:
                magic[r, c] = MAGIC[c - r + 8]
            if abs(c - r) <= 14:
                kinetic[r, c] = KINETIC[abs(c - r)]
    new = np.arange(256)
    py, pz, yy, zz = new // 128, new // 64 % 2, new // 8 % 8, new % 8
    old = (8 * py + yy) * 16 + 8 * pz + zz
    pcol = np.zeros((256, 256))
    pcol[old, new] = 1.0
    prow = np.zeros((256, 256))
    prow[new, (new % 16) * 16 + new // 16] = 1.0
    eye = np.eye(16)
    rm = np.kron(magic, magic).T[old][:, old]
    rk = -0.5 * (np.kron(kinetic, eye) + np.kron(eye, kinetic))[old][:, old]
    lm = np.kron(magic, eye)
    lk = -0.5 * np.kron(kinetic, eye)
    out = [pcol, pcol.T, prow]
    for table in (rm, rk, rm.T, lm, lm.T, lk):
        high = table.astype(np.float32).astype(ml_dtypes.bfloat16)
        out += [high, table - high.astype(np.float64)]
    return np.stack([np.asarray(t, np.float32).astype(ml_dtypes.bfloat16) for t in out])


def offsets(count):
    return (0, 1) if count == 2 else (-1, 0, 1)


def plan(counts):
    start, place, slot_of = 0, {}, []
    for dx in offsets(counts[0]):
        for dy in offsets(counts[1]):
            for dz in offsets(counts[2]):
                if (dx, dy, dz) == (0, 0, 0):
                    continue
                slabs = (1 if dx else 2) * (1 if dy else 2)
                place[(dx, dy, dz)] = start
                slot_of += [len(place)] * slabs
                start += slabs
    total = -(-start // 8) * 8
    slot_of += [0] * (total - start)
    messages = []
    for (dx, dy, dz), first in place.items():
        ex, ey = -dx, -dy
        ez = dz if counts[2] == 2 else -dz
        px, py = (0 if ex < 0 else 1), (0 if ey < 0 else 1)
        if ex and ey:
            messages.append(((ex, ey, ez), (px, pl.ds(py, 1)), first, 1))
        elif ex:
            messages.append(((ex, ey, ez), (px,), first, 2))
        elif ey:
            messages.append(((ex, ey, ez), (slice(None), py), first, 2))
        else:
            messages.append(((ex, ey, ez), (0,), first, 2))
            messages.append(((ex, ey, ez), (1,), first + 2, 2))
    return messages, start, total, slot_of


def mm(a, b):
    return jnp.dot(a, b, preferred_element_type=F32)


def mm_nt(a, b):
    return lax.dot_general(a, b, (((1,), (1,)), ((), ())), preferred_element_type=F32)


def iota(shape, dim):
    return lax.broadcasted_iota(jnp.int32, shape, dim)


def to_octants(value):
    rows = []
    for px in range(2):
        for block in range(4):
            rows.append(
                jnp.concatenate(
                    [
                        value[px * 128 + x * 16 : px * 128 + x * 16 + 16, block * 64 : block * 64 + 64]
                        for x in range(8)
                    ],
                    axis=1,
                )
            )
    return jnp.concatenate(rows, axis=0)


def from_octants(value):
    rows = []
    for px in range(2):
        for x in range(8):
            rows.append(
                jnp.concatenate(
                    [
                        value[(px * 4 + block) * 16 : (px * 4 + block) * 16 + 16, x * 64 : x * 64 + 64]
                        for block in range(4)
                    ],
                    axis=1,
                )
            )
    return jnp.concatenate(rows, axis=0)


def kernel(
    counts, messages, used, slabs,
    box_ref, anchor_ref, pot_ref, tables_hbm, same_hbm,
    out_ref,
    tab, same, ex1, ex2, recv1, recv2,
    halo, hx, hy, hz, hxy, hxz, hyz, hxyz,
    tab_sem, send_sem, recv_sem, halo_send, halo_recv,
):
    me = [lax.axis_index(name) for name in AXES]

    def device(offset):
        return tuple(
            lax.rem(me[i] + (offset[i] + counts[i]), counts[i]) if offset[i] else me[i]
            for i in range(3)
        )

    tab_copy = pltpu.make_async_copy(tables_hbm, tab, tab_sem.at[0])
    same_copy = pltpu.make_async_copy(same_hbm, same, tab_sem.at[1])
    tab_copy.start()
    same_copy.start()

    targets = sorted({m[0] for m in messages})
    barrier = pltpu.get_barrier_semaphore()
    for offset in targets:
        pl.semaphore_signal(barrier, inc=1, device_id=device(offset), device_id_type=MESH)

    z = iota((40, 384), 0)
    lane = iota((40, 384), 1)
    base = lane - ((z // 8) * 64 + z % 8)
    own = None
    for y in range(8):
        picked = jnp.concatenate(
            [pot_ref[pl.ds(by * 8 + y, 40, stride=40), :] for by in range(5)], axis=0
        ).astype(BF)
        part = mm(picked, (base == 8 * y).astype(F32).astype(BF))
        own = part if own is None else own + part
    for by in range(5):
        halo[by] = jnp.concatenate(
            [own[by * 40 : by * 40 + 40], jnp.zeros((8, 384), F32)], axis=0
        ).astype(BF)

    anchor = anchor_ref[...]
    coord = [anchor[:, i : i + 1] for i in range(3)]
    touch = functools.reduce(
        jnp.maximum,
        [((c == 0) | (c == REGION - 1)).astype(F32) for c in coord],
    )
    row_f = iota((16, 128), 0)
    lane_f = iota((16, 128), 1) % 16
    rank = jnp.sum(jnp.where(row_f < lane_f, touch, 0.0), axis=0, keepdims=True)
    touched = jnp.sum(jnp.where(row_f == lane_f, touch, 0.0), axis=0, keepdims=True)
    row_s = iota((64, 128), 0)
    lane_s = iota((64, 128), 1)
    select = jnp.where(
        (row_s // 8 == lane_s // 16) & ((row_s % 8).astype(F32) == rank) & (touched > 0.5), 1.0, 0.0
    ).astype(BF)
    lanes = iota((16, 128), 1)
    hots = []
    for p in range(8):
        hot, first = None, 0
        for i, bit in enumerate((p // 4, p // 2 % 2, p % 2)):
            span = REGION * counts[i]
            value = coord[i] + (me[i] * REGION + bit)
            value = jnp.where(value >= span, value - span, value) + first
            part = (lanes == value).astype(F32)
            hot = part if hot is None else hot + part
            first += span
        hots.append(hot)
    hot = jnp.concatenate(hots, axis=0).astype(BF)

    tab_copy.wait()
    permuted = mm(box_ref[...], tab[PCOL]).astype(BF)
    current_f = mm(tab[PROW], permuted)

    recv1[used:] = jnp.zeros((slabs - used, 16, 640), BF)
    recv2[used:] = jnp.zeros((slabs - used, 16, 512), BF)
    pl.semaphore_wait(barrier, len(targets))

    def halo_copy(n, src, dst, offset):
        return pltpu.make_async_remote_copy(
            src_ref=src, dst_ref=dst, send_sem=halo_send.at[n], recv_sem=halo_recv.at[n],
            device_id=device(offset), device_id_type=MESH,
        )

    low = 1 if counts[2] == 2 else -1
    halos = [
        halo_copy(0, halo.at[:, pl.ds(0, 16), :], hx, (-1, 0, 0)),
        halo_copy(1, halo.at[pl.ds(0, 1)], hy, (0, -1, 0)),
        halo_copy(2, halo.at[:, :, pl.ds(0, 128)], hz, (0, 0, low)),
        halo_copy(3, halo.at[pl.ds(0, 1), pl.ds(0, 16), :], hxy, (-1, -1, 0)),
        halo_copy(4, halo.at[:, pl.ds(0, 16), pl.ds(0, 128)], hxz, (-1, 0, low)),
        halo_copy(5, halo.at[pl.ds(0, 1), :, pl.ds(0, 128)], hyz, (0, -1, low)),
        halo_copy(6, halo.at[pl.ds(0, 1), pl.ds(0, 16), pl.ds(0, 128)], hxyz, (-1, -1, low)),
    ]
    for copy in halos:
        copy.start()

    def exchange(sweep, source, target):
        copies = []
        for n, (offset, index, first, count) in enumerate(messages):
            copies.append(
                pltpu.make_async_remote_copy(
                    src_ref=source.at[index],
                    dst_ref=target.at[pl.ds(first, count)],
                    send_sem=send_sem.at[sweep, n],
                    recv_sem=recv_sem.at[sweep, n],
                    device_id=device(offset),
                    device_id_type=MESH,
                )
            )
        for copy in copies:
            copy.start()
        return copies

    def double(a, b):
        return mm(a, tab[b]) + mm(a, tab[b + 1])

    def double_left(a, b):
        return mm(tab[a], b) + mm(tab[a + 1], b)

    potential = None
    mask_own = mm_nt(hot, hot) > 2.5
    col_o = iota((128, 128), 1) % 16
    same_own = (iota((128, 128), 0) % 16 == col_o).astype(F32).astype(BF)
    delta = jnp.where(iota((16, 128), 0) == iota((16, 128), 1) % 16, PENALTY, 0.0)
    mask_recv = None
    all_copies = list(halos)

    def weights(overlap, mask, table, extra):
        width = overlap.shape[1]
        kept = jnp.where(mask, overlap, 0.0).reshape(8, 16, width).sum(axis=0)
        high = kept.astype(BF)
        rest = (kept - high.astype(F32)).astype(BF)
        coupling = (mm(high, table) + mm(rest, table)) * CELL
        if extra is not None:
            coupling = coupling + extra
        spread = jnp.concatenate([coupling] * 8, axis=0)
        return jnp.where(mask, spread, 0.0).astype(BF)

    for sweep in range(SWEEPS):
        current = current_f.astype(BF)
        octs = to_octants(current_f).astype(BF)
        if sweep == 0:
            ex1[...] = mm(select, jnp.concatenate([octs, hot], axis=1)).astype(BF).reshape(2, 2, 16, 640)
            copies = exchange(0, ex1, recv1)
        else:
            ex2[...] = mm(select, octs).astype(BF).reshape(2, 2, 16, 512)
            copies = exchange(1, ex2, recv2)
        all_copies += copies

        on_grid = double_left(LM, double(current, RM).astype(BF))
        kinetic = double(current, RK) + double_left(LK, current)

        if sweep == 0:
            for copy in halos:
                copy.wait_recv()
            pieces = []
            for by in range(6):
                if by < 5:
                    parts = (halo[by], hx[by], hz[by], hxz[by])
                else:
                    parts = (hy[0], hxy[0], hyz[0], hxyz[0])
                a, b, c, d = [part.astype(F32) for part in parts]
                body = jnp.concatenate([a[:40], b[:8]], axis=0)
                side = jnp.concatenate([c[:40], d[:8]], axis=0)
                pieces.append(
                    jnp.concatenate(
                        [body[:, :256], jnp.concatenate([body[:, 256:320], side[:, :64]], axis=1)], axis=1
                    )
                )
            pieces.append(jnp.zeros((96, 384), F32))
            extended = jnp.concatenate(pieces, axis=0).astype(BF)
            column = iota((16, 384), 1)
            blocks = []
            depth = jnp.concatenate([coord[2]] * 16, axis=0)
            for py in range(2):
                start = (coord[1] + py) * 48 + coord[0] * 8
                rows = jnp.concatenate(
                    [(column == start + x).astype(F32) for x in range(16)], axis=0
                ).astype(BF)
                taken = mm(rows, extended)
                for pz in range(2):
                    block = jnp.zeros((256, 64), F32)
                    for bz in range(5):
                        at = (bz + pz) * 64
                        block = jnp.where(depth == bz, taken[:, at : at + 64], block)
                    blocks.append(block)
            potential = jnp.concatenate(blocks, axis=1)

        weighted = (potential * on_grid).astype(BF)
        applied = double_left(LMT, double(weighted, RMT).astype(BF)) + kinetic
        mixed = to_octants(applied - PENALTY * current_f).astype(BF)
        w_own = weights(mm_nt(mixed, octs), mask_own, same_own, delta)
        correction = mm(w_own, octs)

        if sweep == 0:
            same_copy.wait()
        for copy in copies:
            copy.wait_recv()
        if sweep == 0:
            received = recv1[...].reshape(slabs * 16, 640)
            mask_recv = mm_nt(hot, received[:, 512:]) > 2.5
            cands = received[:, :512]
        else:
            cands = recv2[...].reshape(slabs * 16, 512)
        w_recv = weights(mm_nt(mixed, cands), mask_recv, same[...], None)
        correction = from_octants(correction + mm(w_recv, cands))
        current_f = (current_f - STEP * (applied - correction)).astype(BF).astype(F32)

    back = mm(tab[PROW], current_f.astype(BF)).astype(BF)
    out_ref[...] = mm(back, tab[PCOLT]).astype(BF)
    for copy in all_copies:
        copy.wait_send()


def solution(mesh):
    counts = tuple(mesh.shape[name] for name in AXES)
    messages, used, slabs, slot_of = plan(counts)
    slot = np.repeat(np.array(slot_of), 16)
    item = np.arange(slabs * 16) % 8
    same = (slot[:, None] == slot[None, :]) & (item[:, None] == item[None, :])
    same = same.astype(np.float32).astype(ml_dtypes.bfloat16)
    tables = make_tables()
    vmem = pl.BlockSpec(memory_space=pltpu.VMEM)
    anyspace = pl.BlockSpec(memory_space=pl.ANY)

    def local(boxes, anchors, potential):
        shape = boxes.shape
        out = pl.pallas_call(
            functools.partial(kernel, counts, messages, used, slabs),
            out_shape=jax.ShapeDtypeStruct((256, 256), BF),
            in_specs=[vmem, vmem, vmem, anyspace, anyspace],
            out_specs=vmem,
            scratch_shapes=[
                pltpu.VMEM(tables.shape, BF),
                pltpu.VMEM(same.shape, BF),
                pltpu.VMEM((2, 2, 16, 640), BF),
                pltpu.VMEM((2, 2, 16, 512), BF),
                pltpu.VMEM((slabs, 16, 640), BF),
                pltpu.VMEM((slabs, 16, 512), BF),
                pltpu.VMEM((5, 48, 384), BF),
                pltpu.VMEM((5, 16, 384), BF),
                pltpu.VMEM((1, 48, 384), BF),
                pltpu.VMEM((5, 48, 128), BF),
                pltpu.VMEM((1, 16, 384), BF),
                pltpu.VMEM((5, 16, 128), BF),
                pltpu.VMEM((1, 48, 128), BF),
                pltpu.VMEM((1, 16, 128), BF),
                pltpu.SemaphoreType.DMA((2,)),
                pltpu.SemaphoreType.DMA((SWEEPS, len(messages))),
                pltpu.SemaphoreType.DMA((SWEEPS, len(messages))),
                pltpu.SemaphoreType.DMA((7,)),
                pltpu.SemaphoreType.DMA((7,)),
            ],
            compiler_params=pltpu.CompilerParams(
                collective_id=0, has_side_effects=True, vmem_limit_bytes=40 * 1024 * 1024
            ),
        )(
            boxes.reshape(256, 256),
            anchors.reshape(16, 3),
            potential.reshape(1600, 40),
            jnp.asarray(tables),
            jnp.asarray(same),
        )
        return out.reshape(shape)

    placed = (
        P("gx", "gy", "gz", None, None, None),
        P("gx", "gy", "gz", None, None),
        P("gx", "gy", "gz"),
    )
    return jax.shard_map(
        local,
        mesh=mesh,
        in_specs=placed,
        out_specs=P("gx", "gy", "gz", None, None, None),
        check_vma=False,
    )
```

```python
import functools

import jax
import jax.numpy as jnp
import ml_dtypes
import numpy as np
from jax import lax
from jax.experimental import pallas as pl
from jax.experimental.pallas import tpu as pltpu
from jax.sharding import PartitionSpec as P

REGION = 5
SWEEPS = 2
MAGIC = [
    8.433424733352934e-07,
    -1.290557201342061e-05,
    8.76298447621056e-05,
    -0.00030158038132690465,
    0.001747237136729939,
    -0.009420470302010804,
    0.023738214637249424,
    0.0612625895831208,
    0.9940415697834004,
    -0.06048952891969835,
    -0.021030251609303816,
    0.013372634148547948,
    -0.0034412814449349387,
    0.0004944322768868992,
    -5.185986881173433e-05,
    2.7273449291197967e-06,
]
KINETIC = [
    -3.55369228991319,
    2.2191465938911166,
    -0.6156141465570069,
    0.2371780582153806,
    -0.0822663999742123,
    0.0220702918848226,
    -0.004097656893426338,
    0.00045167920287502236,
    -2.3982285245075998e-05,
    2.0904234952920368e-06,
    -3.7230763047369276e-07,
    -1.0585705549674146e-08,
    -5.8138798302825403e-11,
    2.7080049362631943e-13,
    -6.9244749406392e-18,
]
CELL = 1.0 / 4096.0
STEP = 0.1
PENALTY = 3.0
BF = jnp.bfloat16
F32 = jnp.float32
MESH = pl.DeviceIdType.MESH
AXES = ("gx", "gy", "gz")

PCOL, PCOLT, PROW, RM, RK, RMT, LM, LMT, LK = 0, 1, 2, 3, 5, 7, 9, 11, 13


def make_tables():
    magic = np.zeros((16, 16))
    kinetic = np.zeros((16, 16))
    for r in range(16):
        for c in range(16):
            if -8 <= c - r <= 7:
                magic[r, c] = MAGIC[c - r + 8]
            if abs(c - r) <= 14:
                kinetic[r, c] = KINETIC[abs(c - r)]
    new = np.arange(256)
    py, pz, yy, zz = new // 128, new // 64 % 2, new // 8 % 8, new % 8
    old = (8 * py + yy) * 16 + 8 * pz + zz
    pcol = np.zeros((256, 256))
    pcol[old, new] = 1.0
    prow = np.zeros((256, 256))
    prow[new, (new % 16) * 16 + new // 16] = 1.0
    eye = np.eye(16)
    rm = np.kron(magic, magic).T[old][:, old]
    rk = -0.5 * (np.kron(kinetic, eye) + np.kron(eye, kinetic))[old][:, old]
    lm = np.kron(magic, eye)
    lk = -0.5 * np.kron(kinetic, eye)
    out = [pcol, pcol.T, prow]
    for table in (rm, rk, rm.T, lm, lm.T, lk):
        high = table.astype(np.float32).astype(ml_dtypes.bfloat16)
        out += [high, table - high.astype(np.float64)]
    return np.stack([np.asarray(t, np.float32).astype(ml_dtypes.bfloat16) for t in out])


def plan():
    first, messages, slot_of = 4, [], [0] * 4
    for dx in (-1, 0, 1):
        for dy in (-1, 0, 1):
            if dx == dy == 0:
                continue
            ex, ey = -dx, -dy
            px, py = (0 if ex < 0 else 1), (0 if ey < 0 else 1)
            count = (1 if ex else 2) * (1 if ey else 2)
            if ex and ey:
                index = pl.ds(2 * px + py, 1)
            elif ex:
                index = pl.ds(2 * px, 2)
            else:
                index = None
            messages.append(((ex, ey, 0), index, py, first, count))
            slot_of += [len(messages)] * count
            first += count
    return messages, slot_of


def mm(a, b):
    return jnp.dot(a, b, preferred_element_type=F32)


def mm_nt(a, b):
    return lax.dot_general(a, b, (((1,), (1,)), ((), ())), preferred_element_type=F32)


def iota(shape, dim):
    return lax.broadcasted_iota(jnp.int32, shape, dim)


def to_octants(value):
    rows = []
    for px in range(2):
        for block in range(4):
            rows.append(
                jnp.concatenate(
                    [
                        value[px * 128 + x * 16 : px * 128 + x * 16 + 16, block * 64 : block * 64 + 64]
                        for x in range(8)
                    ],
                    axis=1,
                )
            )
    return jnp.concatenate(rows, axis=0)


def from_octants(value):
    rows = []
    for px in range(2):
        for x in range(8):
            rows.append(
                jnp.concatenate(
                    [
                        value[(px * 4 + block) * 16 : (px * 4 + block) * 16 + 16, x * 64 : x * 64 + 64]
                        for block in range(4)
                    ],
                    axis=1,
                )
            )
    return jnp.concatenate(rows, axis=0)


def kernel(
    counts, messages,
    box_hbm, anchor_hbm, pot_hbm, tables_hbm, same_hbm,
    out_ref,
    box_ref, anchor_ref, pot_ref, tab, same, ex1, ex2, recv1, recv2,
    halo, hx, hy, hz, hxy, hxz, hyz, hxyz,
    load_sem, send_sem, recv_sem, pass_send, pass_recv, halo_send, halo_recv,
):
    me = [lax.axis_index(name) for name in AXES]

    def device(offset):
        return tuple(
            lax.rem(me[i] + (offset[i] + counts[i]), counts[i]) if offset[i] else me[i]
            for i in range(3)
        )

    loads = [
        pltpu.make_async_copy(src, dst, load_sem.at[n])
        for n, (src, dst) in enumerate(
            [
                (anchor_hbm, anchor_ref),
                (box_hbm, box_ref),
                (tables_hbm.at[pl.ds(0, 3)], tab.at[pl.ds(0, 3)]),
                (pot_hbm, pot_ref),
                (tables_hbm.at[pl.ds(3, 12)], tab.at[pl.ds(3, 12)]),
                (same_hbm, same),
            ]
        )
    ]
    for load in loads:
        load.start()

    ups = (1,) if counts[2] == 2 else (-1, 1)
    low = ups[0]
    reach = {m[0] for m in messages} | {(0, 0, up) for up in ups}
    reach |= {(-1, 0, low), (0, -1, low), (-1, -1, low)}
    reach |= {(1, 0, -low), (0, 1, -low), (1, 1, -low)}
    reach = sorted({(x, y, abs(z) if counts[2] == 2 else z) for x, y, z in reach})
    barrier = pltpu.get_barrier_semaphore()
    for offset in reach:
        pl.semaphore_signal(barrier, inc=1, device_id=device(offset), device_id_type=MESH)

    loads[0].wait()
    row_f = iota((16, 128), 0)
    lane_f = iota((16, 128), 1) % 16
    coord = []
    for i in range(3):
        along = anchor_ref[0, 0, i].astype(F32)
        square = jnp.where(iota((16, 16), 0) == iota((16, 16), 1), along, 0.0)
        coord.append(jnp.sum(square, axis=1, keepdims=True).astype(jnp.int32))
    touch = functools.reduce(
        jnp.maximum,
        [((c == 0) | (c == REGION - 1)).astype(F32) for c in coord],
    )
    rank = jnp.sum(jnp.where(row_f < lane_f, touch, 0.0), axis=0, keepdims=True)
    touched = jnp.sum(jnp.where(row_f == lane_f, touch, 0.0), axis=0, keepdims=True)
    row_s = iota((64, 128), 0)
    lane_s = iota((64, 128), 1)
    select = jnp.where(
        (row_s // 8 == lane_s // 16) & ((row_s % 8).astype(F32) == rank) & (touched > 0.5), 1.0, 0.0
    ).astype(BF)
    lanes = iota((16, 128), 1)
    hots = []
    for p in range(8):
        hot, first = None, 0
        for i, bit in enumerate((p // 4, p // 2 % 2, p % 2)):
            span = REGION * counts[i]
            value = coord[i] + (me[i] * REGION + bit)
            value = jnp.where(value >= span, value - span, value) + first
            part = (lanes == value).astype(F32)
            hot = part if hot is None else hot + part
            first += span
        hots.append(hot)
    hot = jnp.concatenate(hots, axis=0).astype(BF)

    loads[1].wait()
    loads[2].wait()
    permuted = mm(box_ref[...], tab[PCOL]).astype(BF)
    current_f = mm(tab[PROW], permuted)

    def remote(src, dst, send, recv, offset):
        return pltpu.make_async_remote_copy(
            src_ref=src, dst_ref=dst, send_sem=send, recv_sem=recv,
            device_id=device(offset), device_id_type=MESH,
        )

    def spread(sweep, source, target):
        copies = []
        for n, (offset, index, py, first, count) in enumerate(messages):
            if index is None:
                pieces = [(pl.ds(py, 1), first, 2 * n), (pl.ds(2 + py, 1), first + 1, 2 * n + 1)]
            else:
                pieces = [(index, first, 2 * n)]
            for where, at, sem in pieces:
                size = count if index is not None else 1
                copies.append(
                    remote(
                        source.at[where], target.at[0, pl.ds(at, size)],
                        send_sem.at[sweep, sem], recv_sem.at[sweep, sem], offset,
                    )
                )
        for copy in copies:
            copy.start()
        own = [
            remote(
                source, target.at[1 + n, pl.ds(0, 4)],
                pass_send.at[sweep, 0, n], pass_recv.at[sweep, 0, n], (0, 0, -up if counts[2] > 2 else up),
            )
            for n, up in enumerate(ups)
        ]
        for copy in own:
            copy.start()
        return copies, own

    def pass_on(sweep, target):
        copies = [
            remote(
                target.at[0, pl.ds(4, 12)], target.at[1 + n, pl.ds(4, 12)],
                pass_send.at[sweep, 1, n], pass_recv.at[sweep, 1, n], (0, 0, -up if counts[2] > 2 else up),
            )
            for n, up in enumerate(ups)
        ]
        for copy in copies:
            copy.start()
        return copies

    def export(sweep, octs):
        if sweep == 0:
            listed = mm(select, jnp.concatenate([octs, hot], axis=1))
            ex1[...] = listed.astype(BF).reshape(4, 16, 640)
            return spread(0, ex1, recv1)
        ex2[...] = mm(select, octs).astype(BF).reshape(4, 16, 512)
        return spread(1, ex2, recv2)

    recv1[0, 0:4] = jnp.zeros((4, 16, 640), BF)
    recv2[0, 0:4] = jnp.zeros((4, 16, 512), BF)
    octs = to_octants(current_f).astype(BF)
    pl.semaphore_wait(barrier, len(reach))
    copies, owns = export(0, octs)

    loads[3].wait()
    z = iota((40, 384), 0)
    lane = iota((40, 384), 1)
    base = lane - ((z // 8) * 64 + z % 8)
    own = None
    for y in range(8):
        picked = jnp.concatenate(
            [pot_ref[pl.ds(by * 8 + y, 40, stride=40), :] for by in range(5)], axis=0
        ).astype(BF)
        part = mm(picked, (base == 8 * y).astype(F32).astype(BF))
        own = part if own is None else own + part
    for by in range(5):
        halo[by] = jnp.concatenate(
            [own[by * 40 : by * 40 + 40], jnp.zeros((8, 384), F32)], axis=0
        ).astype(BF)

    halos = [
        remote(src, dst, halo_send.at[n], halo_recv.at[n], offset)
        for n, (src, dst, offset) in enumerate(
            [
                (halo.at[:, pl.ds(0, 16), :], hx, (-1, 0, 0)),
                (halo.at[pl.ds(0, 1)], hy, (0, -1, 0)),
                (halo.at[:, :, pl.ds(0, 128)], hz, (0, 0, low)),
                (halo.at[pl.ds(0, 1), pl.ds(0, 16), :], hxy, (-1, -1, 0)),
                (halo.at[:, pl.ds(0, 16), pl.ds(0, 128)], hxz, (-1, 0, low)),
                (halo.at[pl.ds(0, 1), :, pl.ds(0, 128)], hyz, (0, -1, low)),
                (halo.at[pl.ds(0, 1), pl.ds(0, 16), pl.ds(0, 128)], hxyz, (-1, -1, low)),
            ]
        )
    ]
    for copy in halos:
        copy.start()

    def double(a, b):
        return mm(a, tab[b]) + mm(a, tab[b + 1])

    def double_left(a, b):
        return mm(tab[a], b) + mm(tab[a + 1], b)

    mask_own = mm_nt(hot, hot) > 2.5
    same_own = (iota((128, 128), 0) % 16 == iota((128, 128), 1) % 16).astype(F32).astype(BF)
    delta = jnp.where(row_f == lane_f, PENALTY, 0.0)
    all_copies = list(halos)

    def weights(overlap, mask, table, extra):
        width = overlap.shape[1]
        kept = jnp.where(mask, overlap, 0.0).reshape(8, 16, width).sum(axis=0)
        high = kept.astype(BF).astype(F32)
        both = mm(jnp.concatenate([high, kept - high], axis=0).astype(BF), table)
        coupling = (both[:16] + both[16:]) * CELL
        if extra is not None:
            coupling = coupling + extra
        copied = jnp.concatenate([coupling] * 8, axis=0)
        return jnp.where(mask, copied, 0.0).astype(BF)

    masks = []
    potential = None
    for sweep in range(SWEEPS):
        current = current_f.astype(BF)
        if sweep:
            octs = to_octants(current_f).astype(BF)
            copies, owns = export(sweep, octs)
        target = recv1 if sweep == 0 else recv2

        if sweep == 0:
            loads[4].wait()
        on_grid = double_left(LM, double(current, RM).astype(BF))
        kinetic = double(current, RK) + double_left(LK, current)

        if sweep == 0:
            for copy in halos:
                copy.wait_recv()
            pieces = []
            for by in range(6):
                if by < 5:
                    parts = (halo[by], hx[by], hz[by], hxz[by])
                else:
                    parts = (hy[0], hxy[0], hyz[0], hxyz[0])
                a, b, c, d = [part.astype(F32) for part in parts]
                body = jnp.concatenate([a[:40], b[:8]], axis=0)
                side = jnp.concatenate([c[:40], d[:8]], axis=0)
                pieces.append(
                    jnp.concatenate(
                        [body[:, :256], jnp.concatenate([body[:, 256:320], side[:, :64]], axis=1)], axis=1
                    )
                )
            pieces.append(jnp.zeros((96, 384), F32))
            extended = jnp.concatenate(pieces, axis=0).astype(BF)
            column = iota((16, 384), 1)
            blocks = []
            depth = jnp.concatenate([coord[2]] * 16, axis=0)
            for py in range(2):
                start = (coord[1] + py) * 48 + coord[0] * 8
                rows = jnp.concatenate(
                    [(column == start + x).astype(F32) for x in range(16)], axis=0
                ).astype(BF)
                taken = mm(rows, extended)
                for pz in range(2):
                    block = jnp.zeros((256, 64), F32)
                    for bz in range(5):
                        at = (bz + pz) * 64
                        block = jnp.where(depth == bz, taken[:, at : at + 64], block)
                    blocks.append(block)
            potential = jnp.concatenate(blocks, axis=1)

        weighted = (potential * on_grid).astype(BF)
        applied = double_left(LMT, double(weighted, RMT).astype(BF)) + kinetic

        for copy in copies:
            copy.wait_recv()
        passed = pass_on(sweep, target)

        mixed = to_octants(applied - PENALTY * current_f).astype(BF)
        w_own = weights(mm_nt(mixed, octs), mask_own, same_own, delta)
        correction = mm(w_own, octs)
        if sweep == 0:
            loads[5].wait()
        for group in range(1 + len(ups)):
            if group == 1:
                for copy in owns + passed:
                    copy.wait_recv()
            received = target[group].reshape(256, target.shape[3])
            if sweep == 0:
                masks.append(mm_nt(hot, received[:, 512:]) > 2.5)
                received = received[:, :512]
            w_near = weights(mm_nt(mixed, received), masks[group], same[...], None)
            correction = correction + mm(w_near, received)
        all_copies += copies + owns + passed
        correction = from_octants(correction)
        current_f = (current_f - STEP * (applied - correction)).astype(BF).astype(F32)

    back = mm(tab[PROW], current_f.astype(BF)).astype(BF)
    out_ref[...] = mm(back, tab[PCOLT]).astype(BF)
    for copy in all_copies:
        copy.wait_send()


def solution(mesh):
    counts = tuple(mesh.shape[name] for name in AXES)
    messages, slot_of = plan()
    slot = np.repeat(np.array(slot_of), 16)
    item = np.arange(256) % 8
    same = (slot[:, None] == slot[None, :]) & (item[:, None] == item[None, :])
    same = same.astype(np.float32).astype(ml_dtypes.bfloat16)
    tables = make_tables()
    layers = 2 if counts[2] == 2 else 3
    vmem = pl.BlockSpec(memory_space=pltpu.VMEM)
    anyspace = pl.BlockSpec(memory_space=pl.ANY)

    def local(boxes, anchors, potential):
        shape = boxes.shape
        out = pl.pallas_call(
            functools.partial(kernel, counts, messages),
            out_shape=jax.ShapeDtypeStruct((256, 256), BF),
            in_specs=[anyspace] * 5,
            out_specs=vmem,
            scratch_shapes=[
                pltpu.VMEM((256, 256), BF),
                pltpu.VMEM((1, 1, 3, 1, 16), jnp.int32),
                pltpu.VMEM((1600, 40), F32),
                pltpu.VMEM(tables.shape, BF),
                pltpu.VMEM(same.shape, BF),
                pltpu.VMEM((4, 16, 640), BF),
                pltpu.VMEM((4, 16, 512), BF),
                pltpu.VMEM((layers, 16, 16, 640), BF),
                pltpu.VMEM((layers, 16, 16, 512), BF),
                pltpu.VMEM((5, 48, 384), BF),
                pltpu.VMEM((5, 16, 384), BF),
                pltpu.VMEM((1, 48, 384), BF),
                pltpu.VMEM((5, 48, 128), BF),
                pltpu.VMEM((1, 16, 384), BF),
                pltpu.VMEM((5, 16, 128), BF),
                pltpu.VMEM((1, 48, 128), BF),
                pltpu.VMEM((1, 16, 128), BF),
                pltpu.SemaphoreType.DMA((6,)),
                pltpu.SemaphoreType.DMA((SWEEPS, 16)),
                pltpu.SemaphoreType.DMA((SWEEPS, 16)),
                pltpu.SemaphoreType.DMA((SWEEPS, 2, 2)),
                pltpu.SemaphoreType.DMA((SWEEPS, 2, 2)),
                pltpu.SemaphoreType.DMA((7,)),
                pltpu.SemaphoreType.DMA((7,)),
            ],
            compiler_params=pltpu.CompilerParams(
                collective_id=0, has_side_effects=True, vmem_limit_bytes=62 * 1024 * 1024
            ),
        )(
            boxes.reshape(256, 256),
            jnp.transpose(anchors, (0, 1, 4, 2, 3)),
            potential.reshape(1600, 40),
            jnp.asarray(tables),
            jnp.asarray(same),
        )
        return out.reshape(shape)

    placed = (
        P("gx", "gy", "gz", None, None, None),
        P("gx", "gy", "gz", None, None),
        P("gx", "gy", "gz"),
    )
    return jax.shard_map(
        local,
        mesh=mesh,
        in_specs=placed,
        out_specs=P("gx", "gy", "gz", None, None, None),
        check_vma=False,
    )
```

```python
import functools

import jax
import jax.numpy as jnp
import ml_dtypes
import numpy as np
from jax import lax
from jax.experimental import pallas as pl
from jax.experimental.pallas import tpu as pltpu
from jax.sharding import PartitionSpec as P

REGION = 5
SWEEPS = 2
MAGIC = [
    8.433424733352934e-07,
    -1.290557201342061e-05,
    8.76298447621056e-05,
    -0.00030158038132690465,
    0.001747237136729939,
    -0.009420470302010804,
    0.023738214637249424,
    0.0612625895831208,
    0.9940415697834004,
    -0.06048952891969835,
    -0.021030251609303816,
    0.013372634148547948,
    -0.0034412814449349387,
    0.0004944322768868992,
    -5.185986881173433e-05,
    2.7273449291197967e-06,
]
KINETIC = [
    -3.55369228991319,
    2.2191465938911166,
    -0.6156141465570069,
    0.2371780582153806,
    -0.0822663999742123,
    0.0220702918848226,
    -0.004097656893426338,
    0.00045167920287502236,
    -2.3982285245075998e-05,
    2.0904234952920368e-06,
    -3.7230763047369276e-07,
    -1.0585705549674146e-08,
    -5.8138798302825403e-11,
    2.7080049362631943e-13,
    -6.9244749406392e-18,
]
CELL = 1.0 / 4096.0
STEP = 0.1
PENALTY = 3.0
BF = jnp.bfloat16
F32 = jnp.float32
MESH = pl.DeviceIdType.MESH
AXES = ("gx", "gy", "gz")

PCOL, PCOLT, PROW, RM, RK, RMT, LM, LMT, LK = range(9)


def rounded(table):
    return table.astype(np.float32).astype(ml_dtypes.bfloat16).astype(np.float64)


def best_scale(table):
    tried = 1.0 + np.arange(2048) / 2048.0
    wrong = [np.square(rounded(table * t) / t - table).sum() for t in tried]
    return tried[int(np.argmin(wrong))]


def make_tables():
    magic = np.zeros((16, 16))
    kinetic = np.zeros((16, 16))
    for r in range(16):
        for c in range(16):
            if -8 <= c - r <= 7:
                magic[r, c] = MAGIC[c - r + 8]
            if abs(c - r) <= 14:
                kinetic[r, c] = KINETIC[abs(c - r)]
    new = np.arange(256)
    py, pz, yy, zz = new // 128, new // 64 % 2, new // 8 % 8, new % 8
    old = (8 * py + yy) * 16 + 8 * pz + zz
    pcol = np.zeros((256, 256))
    pcol[old, new] = 1.0
    prow = np.zeros((256, 256))
    prow[new, (new % 16) * 16 + new // 16] = 1.0
    eye = np.eye(16)
    rm = np.kron(magic, magic).T[old][:, old]
    rk = -0.5 * (np.kron(kinetic, eye) + np.kron(eye, kinetic))[old][:, old]
    lm = np.kron(magic, eye)
    lk = -0.5 * np.kron(kinetic, eye)
    row = slice(7, 8)
    left = best_scale(magic[row])
    right = best_scale(np.kron(magic[row], magic[row]))
    curve = best_scale(np.concatenate([kinetic[row], 2.0 * kinetic[row]]))
    out = [pcol, pcol.T, prow, rm * right, rk * curve, rm.T * right]
    out += [lm * left, lm.T * left, lk * curve]
    stack = np.stack(out).astype(np.float32).astype(ml_dtypes.bfloat16)
    return stack, float((left * right) ** -2), float(1.0 / curve)


def plan():
    first, messages, slot_of = 4, [], [0] * 4
    for dx in (-1, 0, 1):
        for dy in (-1, 0, 1):
            if dx == dy == 0:
                continue
            ex, ey = -dx, -dy
            px, py = (0 if ex < 0 else 1), (0 if ey < 0 else 1)
            count = (1 if ex else 2) * (1 if ey else 2)
            if ex and ey:
                index = pl.ds(2 * px + py, 1)
            elif ex:
                index = pl.ds(2 * px, 2)
            else:
                index = None
            messages.append(((ex, ey, 0), index, py, first, count))
            slot_of += [len(messages)] * count
            first += count
    return messages, slot_of


def mm(a, b):
    return jnp.dot(a, b, preferred_element_type=F32)


def mm_nt(a, b):
    return lax.dot_general(a, b, (((1,), (1,)), ((), ())), preferred_element_type=F32)


def iota(shape, dim):
    return lax.broadcasted_iota(jnp.int32, shape, dim)


def to_octants(value):
    rows = []
    for px in range(2):
        for block in range(4):
            rows.append(
                jnp.concatenate(
                    [
                        value[px * 128 + x * 16 : px * 128 + x * 16 + 16, block * 64 : block * 64 + 64]
                        for x in range(8)
                    ],
                    axis=1,
                )
            )
    return jnp.concatenate(rows, axis=0)


def from_octants(value):
    rows = []
    for px in range(2):
        for x in range(8):
            rows.append(
                jnp.concatenate(
                    [
                        value[(px * 4 + block) * 16 : (px * 4 + block) * 16 + 16, x * 64 : x * 64 + 64]
                        for block in range(4)
                    ],
                    axis=1,
                )
            )
    return jnp.concatenate(rows, axis=0)


def kernel(
    counts, messages, scale_v, scale_k,
    box_hbm, anchor_hbm, pot_hbm, tables_hbm, same_hbm,
    out_ref,
    box_ref, anchor_ref, pot_ref, tab, same, ex1, ex2, recv1, recv2,
    halo, hx, hy, hz, hxy, hxz, hyz, hxyz,
    load_sem, send_sem, recv_sem, pass_send, pass_recv, halo_send, halo_recv,
):
    me = [lax.axis_index(name) for name in AXES]

    def device(offset):
        return tuple(
            lax.rem(me[i] + (offset[i] + counts[i]), counts[i]) if offset[i] else me[i]
            for i in range(3)
        )

    loads = [
        pltpu.make_async_copy(src, dst, load_sem.at[n])
        for n, (src, dst) in enumerate(
            [
                (anchor_hbm, anchor_ref),
                (box_hbm, box_ref),
                (tables_hbm.at[pl.ds(0, 3)], tab.at[pl.ds(0, 3)]),
                (pot_hbm, pot_ref),
                (tables_hbm.at[pl.ds(3, 6)], tab.at[pl.ds(3, 6)]),
                (same_hbm, same),
            ]
        )
    ]
    for load in loads:
        load.start()

    ups = (1,) if counts[2] == 2 else (-1, 1)
    low = ups[0]
    reach = {m[0] for m in messages} | {(0, 0, up) for up in ups}
    reach |= {(-1, 0, low), (0, -1, low), (-1, -1, low)}
    reach |= {(1, 0, -low), (0, 1, -low), (1, 1, -low)}
    reach = sorted({(x, y, abs(z) if counts[2] == 2 else z) for x, y, z in reach})
    barrier = pltpu.get_barrier_semaphore()
    for offset in reach:
        pl.semaphore_signal(barrier, inc=1, device_id=device(offset), device_id_type=MESH)

    loads[3].wait()
    z = iota((40, 384), 0)
    lane = iota((40, 384), 1)
    base = lane - ((z // 8) * 64 + z % 8)
    own = None
    for y in range(8):
        picked = jnp.concatenate(
            [pot_ref[pl.ds(by * 8 + y, 40, stride=40), :] for by in range(5)], axis=0
        ).astype(BF)
        part = mm(picked, (base == 8 * y).astype(F32).astype(BF))
        own = part if own is None else own + part
    for by in range(5):
        halo[by] = jnp.concatenate(
            [own[by * 40 : by * 40 + 40], jnp.zeros((8, 384), F32)], axis=0
        ).astype(BF)

    pl.semaphore_wait(barrier, len(reach))
    def remote(src, dst, send, recv, offset):
        return pltpu.make_async_remote_copy(
            src_ref=src, dst_ref=dst, send_sem=send, recv_sem=recv,
            device_id=device(offset), device_id_type=MESH,
        )

    halos = [
        remote(src, dst, halo_send.at[n], halo_recv.at[n], offset)
        for n, (src, dst, offset) in enumerate(
            [
                (halo.at[:, pl.ds(0, 16), :], hx, (-1, 0, 0)),
                (halo.at[pl.ds(0, 1)], hy, (0, -1, 0)),
                (halo.at[:, :, pl.ds(0, 128)], hz, (0, 0, low)),
                (halo.at[pl.ds(0, 1), pl.ds(0, 16), :], hxy, (-1, -1, 0)),
                (halo.at[:, pl.ds(0, 16), pl.ds(0, 128)], hxz, (-1, 0, low)),
                (halo.at[pl.ds(0, 1), :, pl.ds(0, 128)], hyz, (0, -1, low)),
                (halo.at[pl.ds(0, 1), pl.ds(0, 16), pl.ds(0, 128)], hxyz, (-1, -1, low)),
            ]
        )
    ]
    for copy in halos:
        copy.start()

    loads[0].wait()
    row_f = iota((16, 128), 0)
    lane_f = iota((16, 128), 1) % 16
    coord = []
    for i in range(3):
        along = anchor_ref[0, 0, i].astype(F32)
        square = jnp.where(iota((16, 16), 0) == iota((16, 16), 1), along, 0.0)
        coord.append(jnp.sum(square, axis=1, keepdims=True).astype(jnp.int32))
    touch = functools.reduce(
        jnp.maximum,
        [((c == 0) | (c == REGION - 1)).astype(F32) for c in coord],
    )
    rank = jnp.sum(jnp.where(row_f < lane_f, touch, 0.0), axis=0, keepdims=True)
    touched = jnp.sum(jnp.where(row_f == lane_f, touch, 0.0), axis=0, keepdims=True)
    row_s = iota((64, 128), 0)
    lane_s = iota((64, 128), 1)
    select = jnp.where(
        (row_s // 8 == lane_s // 16) & ((row_s % 8).astype(F32) == rank) & (touched > 0.5), 1.0, 0.0
    ).astype(BF)
    lanes = iota((16, 128), 1)
    hots = []
    for p in range(8):
        hot, first = None, 0
        for i, bit in enumerate((p // 4, p // 2 % 2, p % 2)):
            span = REGION * counts[i]
            value = coord[i] + (me[i] * REGION + bit)
            value = jnp.where(value >= span, value - span, value) + first
            part = (lanes == value).astype(F32)
            hot = part if hot is None else hot + part
            first += span
        hots.append(hot)
    hot = jnp.concatenate(hots, axis=0).astype(BF)

    loads[1].wait()
    loads[2].wait()
    permuted = mm(box_ref[...], tab[PCOL]).astype(BF)
    current_f = mm(tab[PROW], permuted)

    def spread(sweep, source, target):
        copies = []
        for n, (offset, index, py, first, count) in enumerate(messages):
            if index is None:
                pieces = [(pl.ds(py, 1), first, 2 * n), (pl.ds(2 + py, 1), first + 1, 2 * n + 1)]
            else:
                pieces = [(index, first, 2 * n)]
            for where, at, sem in pieces:
                size = count if index is not None else 1
                copies.append(
                    remote(
                        source.at[where], target.at[0, pl.ds(at, size)],
                        send_sem.at[sweep, sem], recv_sem.at[sweep, sem], offset,
                    )
                )
        for copy in copies:
            copy.start()
        own = [
            remote(
                source, target.at[1 + n, pl.ds(0, 4)],
                pass_send.at[sweep, 0, n], pass_recv.at[sweep, 0, n], (0, 0, -up if counts[2] > 2 else up),
            )
            for n, up in enumerate(ups)
        ]
        for copy in own:
            copy.start()
        return copies, own

    def pass_on(sweep, target):
        copies = [
            remote(
                target.at[0, pl.ds(4, 12)], target.at[1 + n, pl.ds(4, 12)],
                pass_send.at[sweep, 1, n], pass_recv.at[sweep, 1, n], (0, 0, -up if counts[2] > 2 else up),
            )
            for n, up in enumerate(ups)
        ]
        for copy in copies:
            copy.start()
        return copies

    def export(sweep, octs):
        if sweep == 0:
            listed = mm(select, jnp.concatenate([octs, hot], axis=1))
            ex1[...] = listed.astype(BF).reshape(4, 16, 640)
            return spread(0, ex1, recv1)
        ex2[...] = mm(select, octs).astype(BF).reshape(4, 16, 512)
        return spread(1, ex2, recv2)

    recv1[0, 0:4] = jnp.zeros((4, 16, 640), BF)
    recv2[0, 0:4] = jnp.zeros((4, 16, 512), BF)
    current = current_f.astype(BF)
    octs_f = to_octants(current_f)
    octs = octs_f.astype(BF)
    copies, owns = export(0, octs)

    mask_own = mm_nt(hot, hot) > 2.5
    same_own = (iota((128, 128), 0) % 16 == iota((128, 128), 1) % 16).astype(F32).astype(BF)
    delta = jnp.where(row_f == lane_f, PENALTY, 0.0)
    all_copies = list(halos)

    def weights(overlap, mask, table, extra):
        width = overlap.shape[1]
        kept = jnp.where(mask, overlap, 0.0).reshape(8, 16, width).sum(axis=0)
        high = kept.astype(BF).astype(F32)
        both = mm(jnp.concatenate([high, kept - high], axis=0).astype(BF), table)
        coupling = (both[:16] + both[16:]) * CELL
        if extra is not None:
            coupling = coupling + extra
        copied = jnp.concatenate([coupling] * 8, axis=0)
        return jnp.where(mask, copied, 0.0).astype(BF)

    masks = []
    potential = None
    for sweep in range(SWEEPS):
        if sweep:
            copies, owns = export(sweep, octs)
            current = from_octants(octs_f).astype(BF)
        target = recv1 if sweep == 0 else recv2

        if sweep == 0:
            loads[4].wait()
        on_grid = mm(tab[LM], mm(current, tab[RM]).astype(BF))
        kinetic = (mm(current, tab[RK]) + mm(tab[LK], current)) * scale_k

        if sweep == 0:
            for copy in halos:
                copy.wait_recv()
            pieces = []
            for by in range(6):
                if by < 5:
                    parts = (halo[by], hx[by], hz[by], hxz[by])
                else:
                    parts = (hy[0], hxy[0], hyz[0], hxyz[0])
                a, b, c, d = [part.astype(F32) for part in parts]
                body = jnp.concatenate([a[:40], b[:8]], axis=0)
                side = jnp.concatenate([c[:40], d[:8]], axis=0)
                pieces.append(
                    jnp.concatenate(
                        [body[:, :256], jnp.concatenate([body[:, 256:320], side[:, :64]], axis=1)], axis=1
                    )
                )
            pieces.append(jnp.zeros((96, 384), F32))
            extended = jnp.concatenate(pieces, axis=0).astype(BF)
            column = iota((16, 384), 1)
            blocks = []
            depth = jnp.concatenate([coord[2]] * 16, axis=0)
            for py in range(2):
                start = (coord[1] + py) * 48 + coord[0] * 8
                rows = jnp.concatenate(
                    [(column == start + x).astype(F32) for x in range(16)], axis=0
                ).astype(BF)
                taken = mm(rows, extended)
                block = taken[:, :128]
                for bz in range(1, 5):
                    block = jnp.where(depth == bz, taken[:, bz * 64 : bz * 64 + 128], block)
                blocks.append(block * scale_v)
            potential = jnp.concatenate(blocks, axis=1)

        weighted = (potential * on_grid).astype(BF)
        applied = mm(tab[LMT], mm(weighted, tab[RMT]).astype(BF)) + kinetic

        applied = to_octants(applied)
        mixed = (applied - PENALTY * octs_f).astype(BF)
        w_own = weights(mm_nt(mixed, octs), mask_own, same_own, delta)
        correction = mm(w_own, octs)
        for copy in copies:
            copy.wait_recv()
        passed = pass_on(sweep, target)
        if sweep == 0:
            loads[5].wait()
        for group in range(1 + len(ups)):
            if group == 1:
                for copy in owns + passed:
                    copy.wait_recv()
            received = target[group].reshape(256, target.shape[3])
            if sweep == 0:
                masks.append(mm_nt(hot, received[:, 512:]) > 2.5)
                received = received[:, :512]
            w_near = weights(mm_nt(mixed, received), masks[group], same[...], None)
            correction = correction + mm(w_near, received)
        all_copies += copies + owns + passed
        octs = (octs_f - STEP * (applied - correction)).astype(BF)
        octs_f = octs.astype(F32)

    back = mm(tab[PROW], from_octants(octs_f).astype(BF)).astype(BF)
    out_ref[...] = mm(back, tab[PCOLT])
    for copy in all_copies:
        copy.wait_send()


def solution(mesh):
    counts = tuple(mesh.shape[name] for name in AXES)
    messages, slot_of = plan()
    slot = np.repeat(np.array(slot_of), 16)
    item = np.arange(256) % 8
    same = (slot[:, None] == slot[None, :]) & (item[:, None] == item[None, :])
    same = same.astype(np.float32).astype(ml_dtypes.bfloat16)
    tables, scale_v, scale_k = make_tables()
    layers = 2 if counts[2] == 2 else 3
    vmem = pl.BlockSpec(memory_space=pltpu.VMEM)
    anyspace = pl.BlockSpec(memory_space=pl.ANY)

    def local(boxes, anchors, potential):
        shape = boxes.shape
        out = pl.pallas_call(
            functools.partial(kernel, counts, messages, scale_v, scale_k),
            out_shape=jax.ShapeDtypeStruct((256, 256), F32),
            in_specs=[anyspace] * 5,
            out_specs=vmem,
            scratch_shapes=[
                pltpu.VMEM((256, 256), BF),
                pltpu.VMEM((1, 1, 3, 1, 16), jnp.int32),
                pltpu.VMEM((1600, 40), F32),
                pltpu.VMEM(tables.shape, BF),
                pltpu.VMEM(same.shape, BF),
                pltpu.VMEM((4, 16, 640), BF),
                pltpu.VMEM((4, 16, 512), BF),
                pltpu.VMEM((layers, 16, 16, 640), BF),
                pltpu.VMEM((layers, 16, 16, 512), BF),
                pltpu.VMEM((5, 48, 384), BF),
                pltpu.VMEM((5, 16, 384), BF),
                pltpu.VMEM((1, 48, 384), BF),
                pltpu.VMEM((5, 48, 128), BF),
                pltpu.VMEM((1, 16, 384), BF),
                pltpu.VMEM((5, 16, 128), BF),
                pltpu.VMEM((1, 48, 128), BF),
                pltpu.VMEM((1, 16, 128), BF),
                pltpu.SemaphoreType.DMA((6,)),
                pltpu.SemaphoreType.DMA((SWEEPS, 16)),
                pltpu.SemaphoreType.DMA((SWEEPS, 16)),
                pltpu.SemaphoreType.DMA((SWEEPS, 2, 2)),
                pltpu.SemaphoreType.DMA((SWEEPS, 2, 2)),
                pltpu.SemaphoreType.DMA((7,)),
                pltpu.SemaphoreType.DMA((7,)),
            ],
            compiler_params=pltpu.CompilerParams(
                collective_id=0, has_side_effects=True, vmem_limit_bytes=62 * 1024 * 1024
            ),
        )(
            boxes.reshape(256, 256),
            jnp.transpose(anchors, (0, 1, 4, 2, 3)),
            potential.reshape(1600, 40),
            jnp.asarray(tables),
            jnp.asarray(same),
        )
        return out.astype(BF).reshape(shape)

    placed = (
        P("gx", "gy", "gz", None, None, None),
        P("gx", "gy", "gz", None, None),
        P("gx", "gy", "gz"),
    )
    return jax.shard_map(
        local,
        mesh=mesh,
        in_specs=placed,
        out_specs=P("gx", "gy", "gz", None, None, None),
        check_vma=False,
    )
```

```python
import functools

import jax
import jax.numpy as jnp
import ml_dtypes
import numpy as np
from jax import lax
from jax.experimental import pallas as pl
from jax.experimental.pallas import tpu as pltpu
from jax.sharding import PartitionSpec as P

REGION = 5
SWEEPS = 2
MAGIC = [
    8.433424733352934e-07,
    -1.290557201342061e-05,
    8.76298447621056e-05,
    -0.00030158038132690465,
    0.001747237136729939,
    -0.009420470302010804,
    0.023738214637249424,
    0.0612625895831208,
    0.9940415697834004,
    -0.06048952891969835,
    -0.021030251609303816,
    0.013372634148547948,
    -0.0034412814449349387,
    0.0004944322768868992,
    -5.185986881173433e-05,
    2.7273449291197967e-06,
]
KINETIC = [
    -3.55369228991319,
    2.2191465938911166,
    -0.6156141465570069,
    0.2371780582153806,
    -0.0822663999742123,
    0.0220702918848226,
    -0.004097656893426338,
    0.00045167920287502236,
    -2.3982285245075998e-05,
    2.0904234952920368e-06,
    -3.7230763047369276e-07,
    -1.0585705549674146e-08,
    -5.8138798302825403e-11,
    2.7080049362631943e-13,
    -6.9244749406392e-18,
]
CELL = 1.0 / 4096.0
STEP = 0.1
PENALTY = 3.0
BF = jnp.bfloat16
F32 = jnp.float32
MESH = pl.DeviceIdType.MESH
AXES = ("gx", "gy", "gz")

PCOL, PCOLT, RM, RK, RMT, LM, LMT, LK = range(8)


def rounded(table):
    return table.astype(np.float32).astype(ml_dtypes.bfloat16).astype(np.float64)


def best_scale(table):
    tried = 1.0 + np.arange(2048) / 2048.0
    wrong = [np.square(rounded(table * t) / t - table).sum() for t in tried]
    return tried[int(np.argmin(wrong))]


def make_tables():
    magic = np.zeros((16, 16))
    kinetic = np.zeros((16, 16))
    for r in range(16):
        for c in range(16):
            if -8 <= c - r <= 7:
                magic[r, c] = MAGIC[c - r + 8]
            if abs(c - r) <= 14:
                kinetic[r, c] = KINETIC[abs(c - r)]
    new = np.arange(256)
    py, pz, yy, zz = new // 128, new // 64 % 2, new // 8 % 8, new % 8
    old = (8 * py + yy) * 16 + 8 * pz + zz
    pcol = np.zeros((256, 256))
    pcol[old, new] = 1.0
    eye = np.eye(16)
    rm = np.kron(magic, magic).T[old][:, old]
    rk = -0.5 * (np.kron(kinetic, eye) + np.kron(eye, kinetic))[old][:, old]
    lm = np.kron(magic, eye)
    lk = -0.5 * np.kron(kinetic, eye)
    row = slice(7, 8)
    left = best_scale(magic[row])
    right = best_scale(np.kron(magic[row], magic[row]))
    curve = best_scale(np.concatenate([kinetic[row], 2.0 * kinetic[row]]))
    out = [pcol, pcol.T, rm * right, rk * curve, rm.T * right]
    out += [lm * left, lm.T * left, lk * curve]
    stack = np.stack(out).astype(np.float32).astype(ml_dtypes.bfloat16)
    return stack, float((left * right) ** -2), float(1.0 / curve)


def plan():
    first, messages, slot_of = 4, [], [0] * 4
    for dx in (-1, 0, 1):
        for dy in (-1, 0, 1):
            if dx == dy == 0:
                continue
            ex, ey = -dx, -dy
            px, py = (0 if ex < 0 else 1), (0 if ey < 0 else 1)
            count = (1 if ex else 2) * (1 if ey else 2)
            if ex and ey:
                index = pl.ds(2 * px + py, 1)
            elif ex:
                index = pl.ds(2 * px, 2)
            else:
                index = None
            messages.append(((ex, ey, 0), index, py, first, count))
            slot_of += [len(messages)] * count
            first += count
    return messages, slot_of


def mm(a, b):
    return jnp.dot(a, b, preferred_element_type=F32)


def mm_nt(a, b):
    return lax.dot_general(a, b, (((1,), (1,)), ((), ())), preferred_element_type=F32)


def iota(shape, dim):
    return lax.broadcasted_iota(jnp.int32, shape, dim)


def to_octants(value):
    rows = []
    for px in range(2):
        for block in range(4):
            rows.append(
                jnp.concatenate(
                    [
                        value[px * 128 + x * 16 : px * 128 + x * 16 + 16, block * 64 : block * 64 + 64]
                        for x in range(8)
                    ],
                    axis=1,
                )
            )
    return jnp.concatenate(rows, axis=0)


def from_octants(value):
    rows = []
    for px in range(2):
        for x in range(8):
            rows.append(
                jnp.concatenate(
                    [
                        value[(px * 4 + block) * 16 : (px * 4 + block) * 16 + 16, x * 64 : x * 64 + 64]
                        for block in range(4)
                    ],
                    axis=1,
                )
            )
    return jnp.concatenate(rows, axis=0)


def kernel(
    counts, messages, scale_v, scale_k,
    box_hbm, anchor_hbm, pot_hbm, tables_hbm, same_hbm,
    out_ref,
    box_ref, anchor_ref, pot_ref, tab, same, ex1, ex2, recv1, recv2,
    turned, halo, hx, hy, hz, hxy, hxz, hyz, hxyz,
    load_sem, send_sem, recv_sem, pass_send, pass_recv, halo_send, halo_recv,
):
    me = [lax.axis_index(name) for name in AXES]

    def device(offset):
        return tuple(
            lax.rem(me[i] + (offset[i] + counts[i]), counts[i]) if offset[i] else me[i]
            for i in range(3)
        )

    loads = [
        pltpu.make_async_copy(src, dst, load_sem.at[n])
        for n, (src, dst) in enumerate(
            [
                (anchor_hbm, anchor_ref),
                (box_hbm, box_ref),
                (tables_hbm.at[pl.ds(0, 2)], tab.at[pl.ds(0, 2)]),
                (pot_hbm, pot_ref),
                (tables_hbm.at[pl.ds(2, 6)], tab.at[pl.ds(2, 6)]),
                (same_hbm, same),
            ]
        )
    ]
    for load in loads:
        load.start()

    ups = (1,) if counts[2] == 2 else (-1, 1)
    low = ups[0]
    reach = {m[0] for m in messages} | {(0, 0, up) for up in ups}
    reach |= {(-1, 0, low), (0, -1, low), (-1, -1, low)}
    reach |= {(1, 0, -low), (0, 1, -low), (1, 1, -low)}
    reach = sorted({(x, y, abs(z) if counts[2] == 2 else z) for x, y, z in reach})
    barrier = pltpu.get_barrier_semaphore()
    for offset in reach:
        pl.semaphore_signal(barrier, inc=1, device_id=device(offset), device_id_type=MESH)

    loads[0].wait()
    row_f = iota((16, 128), 0)
    lane_f = iota((16, 128), 1) % 16
    coord = []
    for i in range(3):
        along = anchor_ref[0, 0, i].astype(F32)
        square = jnp.where(iota((16, 16), 0) == iota((16, 16), 1), along, 0.0)
        coord.append(jnp.sum(square, axis=1, keepdims=True).astype(jnp.int32))
    touch = functools.reduce(
        jnp.maximum,
        [((c == 0) | (c == REGION - 1)).astype(F32) for c in coord],
    )
    rank = jnp.sum(jnp.where(row_f < lane_f, touch, 0.0), axis=0, keepdims=True)
    touched = jnp.sum(jnp.where(row_f == lane_f, touch, 0.0), axis=0, keepdims=True)
    row_s = iota((64, 128), 0)
    lane_s = iota((64, 128), 1)
    select = jnp.where(
        (row_s // 8 == lane_s // 16) & ((row_s % 8).astype(F32) == rank) & (touched > 0.5), 1.0, 0.0
    ).astype(BF)
    lanes = iota((16, 128), 1)
    hots = []
    for p in range(8):
        hot, first = None, 0
        for i, bit in enumerate((p // 4, p // 2 % 2, p % 2)):
            span = REGION * counts[i]
            value = coord[i] + (me[i] * REGION + bit)
            value = jnp.where(value >= span, value - span, value) + first
            part = (lanes == value).astype(F32)
            hot = part if hot is None else hot + part
            first += span
        hots.append(hot)
    hot = jnp.concatenate(hots, axis=0).astype(BF)

    loads[3].wait()
    z = iota((40, 384), 0)
    lane = iota((40, 384), 1)
    base = lane - ((z // 8) * 64 + z % 8)
    own = None
    for y in range(8):
        picked = jnp.concatenate(
            [pot_ref[pl.ds(by * 8 + y, 40, stride=40), :] for by in range(5)], axis=0
        ).astype(BF)
        part = mm(picked, (base == 8 * y).astype(F32).astype(BF))
        own = part if own is None else own + part
    for by in range(5):
        halo[by] = jnp.concatenate(
            [own[by * 40 : by * 40 + 40], jnp.zeros((8, 384), F32)], axis=0
        ).astype(BF)

    pl.semaphore_wait(barrier, len(reach))
    def remote(src, dst, send, recv, offset):
        return pltpu.make_async_remote_copy(
            src_ref=src, dst_ref=dst, send_sem=send, recv_sem=recv,
            device_id=device(offset), device_id_type=MESH,
        )

    halos = [
        remote(src, dst, halo_send.at[n], halo_recv.at[n], offset)
        for n, (src, dst, offset) in enumerate(
            [
                (halo.at[:, pl.ds(0, 16), :], hx, (-1, 0, 0)),
                (halo.at[pl.ds(0, 1)], hy, (0, -1, 0)),
                (halo.at[:, :, pl.ds(0, 128)], hz, (0, 0, low)),
                (halo.at[pl.ds(0, 1), pl.ds(0, 16), :], hxy, (-1, -1, 0)),
                (halo.at[:, pl.ds(0, 16), pl.ds(0, 128)], hxz, (-1, 0, low)),
                (halo.at[pl.ds(0, 1), :, pl.ds(0, 128)], hyz, (0, -1, low)),
                (halo.at[pl.ds(0, 1), pl.ds(0, 16), pl.ds(0, 128)], hxyz, (-1, -1, low)),
            ]
        )
    ]
    for copy in halos:
        copy.start()

    loads[1].wait()
    loads[2].wait()
    permuted = mm(box_ref[...], tab[PCOL])
    halves = []
    for half in range(2):
        turned[half] = permuted[:, half * 128 : half * 128 + 128]
        halves.append(
            jnp.concatenate([turned[half, pl.ds(x, 16, stride=16), :] for x in range(16)], axis=0)
        )
    current_f = jnp.concatenate(halves, axis=1)

    def spread(sweep, source, target):
        copies = []
        for n, (offset, index, py, first, count) in enumerate(messages):
            if index is None:
                pieces = [(pl.ds(py, 1), first, 2 * n), (pl.ds(2 + py, 1), first + 1, 2 * n + 1)]
            else:
                pieces = [(index, first, 2 * n)]
            for where, at, sem in pieces:
                size = count if index is not None else 1
                copies.append(
                    remote(
                        source.at[where], target.at[0, pl.ds(at, size)],
                        send_sem.at[sweep, sem], recv_sem.at[sweep, sem], offset,
                    )
                )
        for copy in copies:
            copy.start()
        own = [
            remote(
                source, target.at[2 * n, pl.ds(0, 4)],
                pass_send.at[sweep, 0, n], pass_recv.at[sweep, 0, n], (0, 0, -up if counts[2] > 2 else up),
            )
            for n, up in enumerate(ups)
        ]
        for copy in own:
            copy.start()
        return copies, own

    def pass_on(sweep, target):
        copies = [
            remote(
                target.at[0, pl.ds(4, 12)], target.at[1 + n, pl.ds(4, 12)],
                pass_send.at[sweep, 1, n], pass_recv.at[sweep, 1, n], (0, 0, -up if counts[2] > 2 else up),
            )
            for n, up in enumerate(ups)
        ]
        for copy in copies:
            copy.start()
        return copies

    def export(sweep, octs):
        if sweep == 0:
            listed = mm(select, jnp.concatenate([octs, hot], axis=1))
            ex1[...] = listed.astype(BF).reshape(4, 16, 640)
            return spread(0, ex1, recv1)
        ex2[...] = mm(select, octs).astype(BF).reshape(4, 16, 512)
        return spread(1, ex2, recv2)

    current = current_f.astype(BF)
    octs_f = to_octants(current_f)
    octs = octs_f.astype(BF)
    copies, owns = export(0, octs)

    mask_own = mm_nt(hot, hot) > 2.5
    same_own = (iota((128, 128), 0) % 16 == iota((128, 128), 1) % 16).astype(F32).astype(BF)
    delta = jnp.where(row_f == lane_f, PENALTY, 0.0)
    all_copies = list(halos)

    def weights(overlap, mask, table, extra):
        width = overlap.shape[1]
        kept = jnp.where(mask, overlap, 0.0).reshape(8, 16, width).sum(axis=0)
        high = kept.astype(BF).astype(F32)
        both = mm(jnp.concatenate([high, kept - high], axis=0).astype(BF), table)
        coupling = (both[:16] + both[16:]) * CELL
        if extra is not None:
            coupling = coupling + extra
        copied = jnp.concatenate([coupling] * 8, axis=0)
        return jnp.where(mask, copied, 0.0).astype(BF)

    masks = []
    potential = None
    for sweep in range(SWEEPS):
        if sweep:
            copies, owns = export(sweep, octs)
            current = from_octants(octs_f).astype(BF)
        target = recv1 if sweep == 0 else recv2

        if sweep == 0:
            loads[4].wait()
        on_grid = mm(tab[LM], mm(current, tab[RM]).astype(BF))
        kinetic = (mm(current, tab[RK]) + mm(tab[LK], current)) * scale_k

        if sweep == 0:
            for copy in halos:
                copy.wait_recv()
            pieces = []
            for by in range(6):
                if by < 5:
                    parts = (halo[by], hx[by], hz[by], hxz[by])
                else:
                    parts = (hy[0], hxy[0], hyz[0], hxyz[0])
                a, b, c, d = [part.astype(F32) for part in parts]
                body = jnp.concatenate([a[:40], b[:8]], axis=0)
                side = jnp.concatenate([c[:40], d[:8]], axis=0)
                pieces.append(
                    jnp.concatenate(
                        [body[:, :256], jnp.concatenate([body[:, 256:320], side[:, :64]], axis=1)], axis=1
                    )
                )
            pieces.append(jnp.zeros((96, 384), F32))
            extended = jnp.concatenate(pieces, axis=0).astype(BF)
            column = iota((16, 384), 1)
            blocks = []
            depth = jnp.concatenate([coord[2]] * 16, axis=0)
            for py in range(2):
                start = (coord[1] + py) * 48 + coord[0] * 8
                rows = jnp.concatenate(
                    [(column == start + x).astype(F32) for x in range(16)], axis=0
                ).astype(BF)
                taken = mm(rows, extended)
                block = taken[:, :128]
                for bz in range(1, 5):
                    block = jnp.where(depth == bz, taken[:, bz * 64 : bz * 64 + 128], block)
                blocks.append(block * scale_v)
            potential = jnp.concatenate(blocks, axis=1)

        if sweep == 0:
            for copy in copies:
                copy.wait_recv()
            passed = pass_on(sweep, target)
        weighted = (potential * on_grid).astype(BF)
        applied = mm(tab[LMT], mm(weighted, tab[RMT]).astype(BF)) + kinetic

        if sweep == 0:
            for copy in owns + passed:
                copy.wait_recv()
            loads[5].wait()
        applied = to_octants(applied)
        mixed = (applied - PENALTY * octs_f).astype(BF)
        w_own = weights(mm_nt(mixed, octs), mask_own, same_own, delta)
        correction = mm(w_own, octs)
        if sweep:
            for copy in copies:
                copy.wait_recv()
            passed = pass_on(sweep, target)
            for copy in owns:
                copy.wait_recv()
        for group in range(1 + len(ups)):
            if group == 1 and sweep:
                for copy in passed:
                    copy.wait_recv()
            skip = 4 if group == 1 else 0
            received = target[group, skip:].reshape(256 - skip * 16, target.shape[3])
            if sweep == 0:
                masks.append(mm_nt(hot, received[:, 512:]) > 2.5)
            received = received[:, :512]
            w_near = weights(mm_nt(mixed, received), masks[group], same[skip * 16 :, skip * 16 :], None)
            correction = correction + mm(w_near, received)
        all_copies += copies + owns + passed
        octs = (octs_f - STEP * (applied - correction)).astype(BF)
        octs_f = octs.astype(F32)

    back = mm(from_octants(octs_f).astype(BF), tab[PCOLT])
    for half in range(2):
        for x in range(16):
            turned[half, pl.ds(x, 16, stride=16), :] = back[
                x * 16 : x * 16 + 16, half * 128 : half * 128 + 128
            ]
    out_ref[...] = jnp.concatenate([turned[0], turned[1]], axis=1).astype(BF)
    for copy in all_copies:
        copy.wait_send()


def solution(mesh):
    counts = tuple(mesh.shape[name] for name in AXES)
    messages, slot_of = plan()
    slot = np.repeat(np.array(slot_of), 16)
    item = np.arange(256) % 8
    same = (slot[:, None] == slot[None, :]) & (item[:, None] == item[None, :])
    same = same.astype(np.float32).astype(ml_dtypes.bfloat16)
    tables, scale_v, scale_k = make_tables()
    layers = 2 if counts[2] == 2 else 3
    vmem = pl.BlockSpec(memory_space=pltpu.VMEM)
    anyspace = pl.BlockSpec(memory_space=pl.ANY)

    def local(boxes, anchors, potential):
        shape = boxes.shape
        out = pl.pallas_call(
            functools.partial(kernel, counts, messages, scale_v, scale_k),
            out_shape=jax.ShapeDtypeStruct((256, 256), BF),
            in_specs=[anyspace] * 5,
            out_specs=vmem,
            scratch_shapes=[
                pltpu.VMEM((256, 256), BF),
                pltpu.VMEM((1, 1, 3, 1, 16), jnp.int32),
                pltpu.VMEM((1600, 40), F32),
                pltpu.VMEM(tables.shape, BF),
                pltpu.VMEM(same.shape, BF),
                pltpu.VMEM((4, 16, 640), BF),
                pltpu.VMEM((4, 16, 512), BF),
                pltpu.VMEM((layers, 16, 16, 640), BF),
                pltpu.VMEM((layers, 16, 16, 512), BF),
                pltpu.VMEM((2, 256, 128), F32),
                pltpu.VMEM((5, 48, 384), BF),
                pltpu.VMEM((5, 16, 384), BF),
                pltpu.VMEM((1, 48, 384), BF),
                pltpu.VMEM((5, 48, 128), BF),
                pltpu.VMEM((1, 16, 384), BF),
                pltpu.VMEM((5, 16, 128), BF),
                pltpu.VMEM((1, 48, 128), BF),
                pltpu.VMEM((1, 16, 128), BF),
                pltpu.SemaphoreType.DMA((6,)),
                pltpu.SemaphoreType.DMA((SWEEPS, 16)),
                pltpu.SemaphoreType.DMA((SWEEPS, 16)),
                pltpu.SemaphoreType.DMA((SWEEPS, 2, 2)),
                pltpu.SemaphoreType.DMA((SWEEPS, 2, 2)),
                pltpu.SemaphoreType.DMA((7,)),
                pltpu.SemaphoreType.DMA((7,)),
            ],
            compiler_params=pltpu.CompilerParams(
                collective_id=0, has_side_effects=True, vmem_limit_bytes=55040 * 1024
            ),
        )(
            boxes.reshape(256, 256),
            jnp.transpose(anchors, (0, 1, 4, 2, 3)),
            potential.reshape(1600, 40),
            jnp.asarray(tables),
            jnp.asarray(same),
        )
        return out.reshape(shape)

    placed = (
        P("gx", "gy", "gz", None, None, None),
        P("gx", "gy", "gz", None, None),
        P("gx", "gy", "gz"),
    )
    return jax.shard_map(
        local,
        mesh=mesh,
        in_specs=placed,
        out_specs=P("gx", "gy", "gz", None, None, None),
        check_vma=False,
    )
```

```python
import functools

import jax
import jax.numpy as jnp
import ml_dtypes
import numpy as np
from jax import lax
from jax.experimental import pallas as pl
from jax.experimental.pallas import tpu as pltpu
from jax.sharding import PartitionSpec as P

REGION = 5
SWEEPS = 2
MAGIC = [
    8.433424733352934e-07,
    -1.290557201342061e-05,
    8.76298447621056e-05,
    -0.00030158038132690465,
    0.001747237136729939,
    -0.009420470302010804,
    0.023738214637249424,
    0.0612625895831208,
    0.9940415697834004,
    -0.06048952891969835,
    -0.021030251609303816,
    0.013372634148547948,
    -0.0034412814449349387,
    0.0004944322768868992,
    -5.185986881173433e-05,
    2.7273449291197967e-06,
]
KINETIC = [
    -3.55369228991319,
    2.2191465938911166,
    -0.6156141465570069,
    0.2371780582153806,
    -0.0822663999742123,
    0.0220702918848226,
    -0.004097656893426338,
    0.00045167920287502236,
    -2.3982285245075998e-05,
    2.0904234952920368e-06,
    -3.7230763047369276e-07,
    -1.0585705549674146e-08,
    -5.8138798302825403e-11,
    2.7080049362631943e-13,
    -6.9244749406392e-18,
]
CELL = 1.0 / 4096.0
STEP = 0.1
PENALTY = 3.0
BF = jnp.bfloat16
F32 = jnp.float32
MESH = pl.DeviceIdType.MESH
CYCLE = ((0, 0), (0, 1), (1, 1), (1, 0))
AXES = ("gx", "gy", "gz")

PCOL, PCOLT, RM, RK, RMT, LM, LMT, LK = range(8)


def rounded(table):
    return table.astype(np.float32).astype(ml_dtypes.bfloat16).astype(np.float64)


def best_scale(table):
    tried = 1.0 + np.arange(2048) / 2048.0
    wrong = [np.square(rounded(table * t) / t - table).sum() for t in tried]
    return tried[int(np.argmin(wrong))]


def make_tables():
    magic = np.zeros((16, 16))
    kinetic = np.zeros((16, 16))
    for r in range(16):
        for c in range(16):
            if -8 <= c - r <= 7:
                magic[r, c] = MAGIC[c - r + 8]
            if abs(c - r) <= 14:
                kinetic[r, c] = KINETIC[abs(c - r)]
    new = np.arange(256)
    py, pz, yy, zz = new // 128, new // 64 % 2, new // 8 % 8, new % 8
    old = (8 * py + yy) * 16 + 8 * pz + zz
    pcol = np.zeros((256, 256))
    pcol[old, new] = 1.0
    eye = np.eye(16)
    rm = np.kron(magic, magic).T[old][:, old]
    rk = -0.5 * (np.kron(kinetic, eye) + np.kron(eye, kinetic))[old][:, old]
    lm = np.kron(magic, eye)
    lk = -0.5 * np.kron(kinetic, eye)
    row = slice(7, 8)
    left = best_scale(magic[row])
    right = best_scale(np.kron(magic[row], magic[row]))
    curve = best_scale(np.concatenate([kinetic[row], 2.0 * kinetic[row]]))
    out = [pcol, pcol.T, rm * right, rk * curve, rm.T * right]
    out += [lm * left, lm.T * left, lk * curve]
    stack = np.stack(out).astype(np.float32).astype(ml_dtypes.bfloat16)
    return stack, float((left * right) ** -2), float(1.0 / curve)


def plan():
    first, messages, slot_of = 4, [], [0] * 4
    for dx in (-1, 0, 1):
        for dy in (-1, 0, 1):
            if dx == dy == 0:
                continue
            ex, ey = -dx, -dy
            px, py = (0 if ex < 0 else 1), (0 if ey < 0 else 1)
            count = (1 if ex else 2) * (1 if ey else 2)
            if ex and ey:
                index = CYCLE.index((px, py))
            elif ex:
                index = 2 * px
            else:
                index = 1 if py else 3
            messages.append(((ex, ey, 0), index, first, count))
            slot_of += [len(messages)] * count
            first += count
    return messages, slot_of


def mm(a, b):
    return jnp.dot(a, b, preferred_element_type=F32)


def mm_nt(a, b):
    return lax.dot_general(a, b, (((1,), (1,)), ((), ())), preferred_element_type=F32)


def iota(shape, dim):
    return lax.broadcasted_iota(jnp.int32, shape, dim)


def to_octants(value):
    rows = []
    for px in range(2):
        for block in range(4):
            rows.append(
                jnp.concatenate(
                    [
                        value[px * 128 + x * 16 : px * 128 + x * 16 + 16, block * 64 : block * 64 + 64]
                        for x in range(8)
                    ],
                    axis=1,
                )
            )
    return jnp.concatenate(rows, axis=0)


def from_octants(value):
    rows = []
    for px in range(2):
        for x in range(8):
            rows.append(
                jnp.concatenate(
                    [
                        value[(px * 4 + block) * 16 : (px * 4 + block) * 16 + 16, x * 64 : x * 64 + 64]
                        for block in range(4)
                    ],
                    axis=1,
                )
            )
    return jnp.concatenate(rows, axis=0)


def kernel(
    counts, messages, scale_v, scale_k,
    box_hbm, anchor_ref, pot_hbm, tables_hbm, same_hbm,
    out_ref,
    box_ref, pot_ref, tab, same, ex1, ex2, recv1, recv2,
    turned, halo, hx, hy, hz, hxy, hxz, hyz, hxyz,
    load_sem, send_sem, recv_sem, pass_send, pass_recv, halo_send, halo_recv,
):
    me = [lax.axis_index(name) for name in AXES]

    def device(offset):
        return tuple(
            lax.rem(me[i] + (offset[i] + counts[i]), counts[i]) if offset[i] else me[i]
            for i in range(3)
        )

    ups = (1,) if counts[2] == 2 else (-1, 1)
    low = ups[0]
    reach = {m[0] for m in messages} | {(0, 0, up) for up in ups}
    reach |= {(-1, 0, low), (0, -1, low), (-1, -1, low)}
    reach |= {(1, 0, -low), (0, 1, -low), (1, 1, -low)}
    reach = sorted({(x, y, abs(z) if counts[2] == 2 else z) for x, y, z in reach})
    barrier = pltpu.get_barrier_semaphore()
    for offset in reach:
        pl.semaphore_signal(barrier, inc=1, device_id=device(offset), device_id_type=MESH)

    loads = [
        pltpu.make_async_copy(src, dst, load_sem.at[n])
        for n, (src, dst) in enumerate(
            [
                (pot_hbm, pot_ref),
                (box_hbm, box_ref),
                (tables_hbm.at[pl.ds(0, 2)], tab.at[pl.ds(0, 2)]),
                (tables_hbm.at[pl.ds(2, 6)], tab.at[pl.ds(2, 6)]),
                (same_hbm, same),
            ]
        )
    ]
    for load in loads:
        load.start()

    row_f = iota((16, 128), 0)
    lane_f = iota((16, 128), 1) % 16
    coord = []
    for i in range(3):
        along = anchor_ref[0, 0, i].astype(F32)
        square = jnp.where(iota((16, 16), 0) == iota((16, 16), 1), along, 0.0)
        coord.append(jnp.sum(square, axis=1, keepdims=True).astype(jnp.int32))
    touch = functools.reduce(
        jnp.maximum,
        [((c == 0) | (c == REGION - 1)).astype(F32) for c in coord],
    )
    rank = jnp.sum(jnp.where(row_f < lane_f, touch, 0.0), axis=0, keepdims=True)
    touched = jnp.sum(jnp.where(row_f == lane_f, touch, 0.0), axis=0, keepdims=True)
    row_s = iota((80, 128), 0)
    lane_s = iota((80, 128), 1)
    slab = row_s // 16
    octant = jnp.where(slab == 4, 0, jnp.where(slab == 2, 3, jnp.where(slab == 3, 2, slab)))
    octant = octant * 2 + row_s // 8 % 2
    select = jnp.where(
        (octant == lane_s // 16) & ((row_s % 8).astype(F32) == rank) & (touched > 0.5), 1.0, 0.0
    ).astype(BF)
    lanes = iota((16, 128), 1)
    hots = []
    for p in range(8):
        hot, first = None, 0
        for i, bit in enumerate((p // 4, p // 2 % 2, p % 2)):
            span = REGION * counts[i]
            value = coord[i] + (me[i] * REGION + bit)
            value = jnp.where(value >= span, value - span, value) + first
            part = (lanes == value).astype(F32)
            hot = part if hot is None else hot + part
            first += span
        hots.append(hot)
    hot = jnp.concatenate(hots, axis=0).astype(BF)

    loads[0].wait()
    z = iota((40, 384), 0)
    lane = iota((40, 384), 1)
    base = lane - ((z // 8) * 64 + z % 8)
    own = None
    for y in range(8):
        picked = jnp.concatenate(
            [pot_ref[pl.ds(by * 8 + y, 40, stride=40), :] for by in range(5)], axis=0
        ).astype(BF)
        part = mm(picked, (base == 8 * y).astype(F32).astype(BF))
        own = part if own is None else own + part
    for by in range(5):
        halo[by] = jnp.concatenate(
            [own[by * 40 : by * 40 + 40], jnp.zeros((8, 384), F32)], axis=0
        ).astype(BF)

    pl.semaphore_wait(barrier, len(reach))
    def remote(src, dst, send, recv, offset):
        return pltpu.make_async_remote_copy(
            src_ref=src, dst_ref=dst, send_sem=send, recv_sem=recv,
            device_id=device(offset), device_id_type=MESH,
        )

    halos = [
        remote(src, dst, halo_send.at[n], halo_recv.at[n], offset)
        for n, (src, dst, offset) in enumerate(
            [
                (halo.at[:, pl.ds(0, 16), :], hx, (-1, 0, 0)),
                (halo.at[pl.ds(0, 1)], hy, (0, -1, 0)),
                (halo.at[:, :, pl.ds(0, 128)], hz, (0, 0, low)),
                (halo.at[pl.ds(0, 1), pl.ds(0, 16), :], hxy, (-1, -1, 0)),
                (halo.at[:, pl.ds(0, 16), pl.ds(0, 128)], hxz, (-1, 0, low)),
                (halo.at[pl.ds(0, 1), :, pl.ds(0, 128)], hyz, (0, -1, low)),
                (halo.at[pl.ds(0, 1), pl.ds(0, 16), pl.ds(0, 128)], hxyz, (-1, -1, low)),
            ]
        )
    ]
    for copy in halos:
        copy.start()

    loads[1].wait()
    loads[2].wait()
    permuted = mm(box_ref[...], tab[PCOL])
    halves = []
    for half in range(2):
        turned[half] = permuted[:, half * 128 : half * 128 + 128]
        halves.append(
            jnp.concatenate([turned[half, pl.ds(x, 16, stride=16), :] for x in range(16)], axis=0)
        )
    current_f = jnp.concatenate(halves, axis=1)

    def spread(sweep, source, target):
        for offset, index, first, count in messages:
            remote(
                source.at[pl.ds(index, count)], target.at[0, pl.ds(first, count)],
                send_sem.at[sweep], recv_sem.at[sweep], offset,
            ).start()
        landed = target.at[0, pl.ds(4, 12)]
        copies = [remote(landed, landed, send_sem.at[sweep], recv_sem.at[sweep], (1, 0, 0))]
        own = [
            remote(
                source.at[pl.ds(0, 4)], target.at[2 * n, pl.ds(0, 4)],
                pass_send.at[sweep, 0, n], pass_recv.at[sweep, 0, n], (0, 0, -up if counts[2] > 2 else up),
            )
            for n, up in enumerate(ups)
        ]
        for copy in own:
            copy.start()
        return copies, own

    def pass_on(sweep, target):
        copies = [
            remote(
                target.at[0, pl.ds(4, 12)], target.at[1 + n, pl.ds(4, 12)],
                pass_send.at[sweep, 1, n], pass_recv.at[sweep, 1, n], (0, 0, -up if counts[2] > 2 else up),
            )
            for n, up in enumerate(ups)
        ]
        for copy in copies:
            copy.start()
        return copies

    def export(sweep, octs):
        if sweep == 0:
            listed = mm(select, jnp.concatenate([octs, hot], axis=1))
            ex1[...] = listed.astype(BF).reshape(5, 16, 640)
            return spread(0, ex1, recv1)
        ex2[...] = mm(select, octs).astype(BF).reshape(5, 16, 512)
        return spread(1, ex2, recv2)

    current = current_f.astype(BF)
    octs_f = to_octants(current_f)
    octs = octs_f.astype(BF)
    copies, owns = export(0, octs)

    mask_own = mm_nt(hot, hot) > 2.5
    same_own = (iota((128, 128), 0) % 16 == iota((128, 128), 1) % 16).astype(F32).astype(BF)
    delta = jnp.where(row_f == lane_f, PENALTY, 0.0)
    sent = list(halos)

    def weights(overlap, mask, table, extra):
        width = overlap.shape[1]
        kept = jnp.where(mask, overlap, 0.0).reshape(8, 16, width).sum(axis=0)
        high = kept.astype(BF).astype(F32)
        both = mm(jnp.concatenate([high, kept - high], axis=0).astype(BF), table)
        coupling = (both[:16] + both[16:]) * CELL
        if extra is not None:
            coupling = coupling + extra
        copied = jnp.concatenate([coupling] * 8, axis=0)
        return jnp.where(mask, copied, 0.0).astype(BF)

    masks = []
    potential = None
    for sweep in range(SWEEPS):
        if sweep:
            copies, owns = export(sweep, octs)
            current = from_octants(octs_f).astype(BF)
        target = recv1 if sweep == 0 else recv2

        if sweep == 0:
            loads[3].wait()
        on_grid = mm(tab[LM], mm(current, tab[RM]).astype(BF))
        kinetic = (mm(current, tab[RK]) + mm(tab[LK], current)) * scale_k

        if sweep == 0:
            for copy in halos:
                copy.wait_recv()
            pieces = []
            for by in range(6):
                if by < 5:
                    parts = (halo[by], hx[by], hz[by], hxz[by])
                else:
                    parts = (hy[0], hxy[0], hyz[0], hxyz[0])
                a, b, c, d = [part.astype(F32) for part in parts]
                body = jnp.concatenate([a[:40], b[:8]], axis=0)
                side = jnp.concatenate([c[:40], d[:8]], axis=0)
                pieces.append(
                    jnp.concatenate(
                        [body[:, :256], jnp.concatenate([body[:, 256:320], side[:, :64]], axis=1)], axis=1
                    )
                )
            pieces.append(jnp.zeros((96, 384), F32))
            extended = jnp.concatenate(pieces, axis=0).astype(BF)
            column = iota((16, 384), 1)
            blocks = []
            depth = jnp.concatenate([coord[2]] * 16, axis=0)
            for py in range(2):
                start = (coord[1] + py) * 48 + coord[0] * 8
                rows = jnp.concatenate(
                    [(column == start + x).astype(F32) for x in range(16)], axis=0
                ).astype(BF)
                taken = mm(rows, extended)
                block = taken[:, :128]
                for bz in range(1, 5):
                    block = jnp.where(depth == bz, taken[:, bz * 64 : bz * 64 + 128], block)
                blocks.append(block * scale_v)
            potential = jnp.concatenate(blocks, axis=1)

        if sweep == 0:
            for copy in copies:
                copy.wait_recv()
            passed = pass_on(sweep, target)
        weighted = (potential * on_grid).astype(BF)
        applied = mm(tab[LMT], mm(weighted, tab[RMT]).astype(BF)) + kinetic

        if sweep == 0:
            for copy in owns + passed:
                copy.wait_recv()
            loads[4].wait()
        applied = to_octants(applied)
        mixed = (applied - PENALTY * octs_f).astype(BF)
        w_own = weights(mm_nt(mixed, octs), mask_own, same_own, delta)
        correction = mm(w_own, octs)
        if sweep:
            for copy in sent:
                copy.wait_send()
            for copy in copies:
                copy.wait_recv()
            passed = pass_on(sweep, target)
            for copy in owns:
                copy.wait_recv()
        for group in range(1 + len(ups)):
            if group == 1 and sweep:
                for copy in copies + owns + passed:
                    copy.wait_send()
                for copy in passed:
                    copy.wait_recv()
            skip = 4 if group == 1 else 0
            received = target[group, skip:].reshape(256 - skip * 16, target.shape[3])
            if sweep == 0:
                masks.append(mm_nt(hot, received[:, 512:]) > 2.5)
            received = received[:, :512]
            w_near = weights(mm_nt(mixed, received), masks[group], same[skip * 16 :, skip * 16 :], None)
            correction = correction + mm(w_near, received)
        if sweep == 0:
            sent += copies + owns + passed
        octs = (octs_f - STEP * (applied - correction)).astype(BF)
        octs_f = octs.astype(F32)

    back = mm(from_octants(octs_f).astype(BF), tab[PCOLT])
    for half in range(2):
        for x in range(16):
            turned[half, pl.ds(x, 16, stride=16), :] = back[
                x * 16 : x * 16 + 16, half * 128 : half * 128 + 128
            ]
    out_ref[...] = jnp.concatenate([turned[0], turned[1]], axis=1).astype(BF)


def solution(mesh):
    counts = tuple(mesh.shape[name] for name in AXES)
    messages, slot_of = plan()
    slot = np.repeat(np.array(slot_of), 16)
    item = np.arange(256) % 8
    same = (slot[:, None] == slot[None, :]) & (item[:, None] == item[None, :])
    same = same.astype(np.float32).astype(ml_dtypes.bfloat16)
    tables, scale_v, scale_k = make_tables()
    layers = 2 if counts[2] == 2 else 3
    vmem = pl.BlockSpec(memory_space=pltpu.VMEM)
    anyspace = pl.BlockSpec(memory_space=pl.ANY)

    def local(boxes, anchors, potential):
        shape = boxes.shape
        out = pl.pallas_call(
            functools.partial(kernel, counts, messages, scale_v, scale_k),
            out_shape=jax.ShapeDtypeStruct((256, 256), BF),
            in_specs=[anyspace, vmem, anyspace, anyspace, anyspace],
            out_specs=vmem,
            scratch_shapes=[
                pltpu.VMEM((256, 256), BF),
                pltpu.VMEM((1600, 40), F32),
                pltpu.VMEM(tables.shape, BF),
                pltpu.VMEM(same.shape, BF),
                pltpu.VMEM((5, 16, 640), BF),
                pltpu.VMEM((5, 16, 512), BF),
                pltpu.VMEM((layers, 16, 16, 640), BF),
                pltpu.VMEM((layers, 16, 16, 512), BF),
                pltpu.VMEM((2, 256, 128), F32),
                pltpu.VMEM((5, 48, 384), BF),
                pltpu.VMEM((5, 16, 384), BF),
                pltpu.VMEM((1, 48, 384), BF),
                pltpu.VMEM((5, 48, 128), BF),
                pltpu.VMEM((1, 16, 384), BF),
                pltpu.VMEM((5, 16, 128), BF),
                pltpu.VMEM((1, 48, 128), BF),
                pltpu.VMEM((1, 16, 128), BF),
                pltpu.SemaphoreType.DMA((5,)),
                pltpu.SemaphoreType.DMA((SWEEPS,)),
                pltpu.SemaphoreType.DMA((SWEEPS,)),
                pltpu.SemaphoreType.DMA((SWEEPS, 2, 2)),
                pltpu.SemaphoreType.DMA((SWEEPS, 2, 2)),
                pltpu.SemaphoreType.DMA((7,)),
                pltpu.SemaphoreType.DMA((7,)),
            ],
            compiler_params=pltpu.CompilerParams(
                collective_id=0, has_side_effects=True, vmem_limit_bytes=55040 * 1024
            ),
        )(
            boxes.reshape(256, 256),
            jnp.transpose(anchors, (0, 1, 4, 2, 3)),
            potential.reshape(1600, 40),
            jnp.asarray(tables),
            jnp.asarray(same),
        )
        return out.reshape(shape)

    placed = (
        P("gx", "gy", "gz", None, None, None),
        P("gx", "gy", "gz", None, None),
        P("gx", "gy", "gz"),
    )
    return jax.shard_map(
        local,
        mesh=mesh,
        in_specs=placed,
        out_specs=P("gx", "gy", "gz", None, None, None),
        check_vma=False,
    )
```

```python
import functools

import jax
import jax.numpy as jnp
import ml_dtypes
import numpy as np
from jax import lax
from jax.experimental import pallas as pl
from jax.experimental.pallas import tpu as pltpu
from jax.sharding import PartitionSpec as P

REGION = 5
SWEEPS = 2
MAGIC = [
    8.433424733352934e-07,
    -1.290557201342061e-05,
    8.76298447621056e-05,
    -0.00030158038132690465,
    0.001747237136729939,
    -0.009420470302010804,
    0.023738214637249424,
    0.0612625895831208,
    0.9940415697834004,
    -0.06048952891969835,
    -0.021030251609303816,
    0.013372634148547948,
    -0.0034412814449349387,
    0.0004944322768868992,
    -5.185986881173433e-05,
    2.7273449291197967e-06,
]
KINETIC = [
    -3.55369228991319,
    2.2191465938911166,
    -0.6156141465570069,
    0.2371780582153806,
    -0.0822663999742123,
    0.0220702918848226,
    -0.004097656893426338,
    0.00045167920287502236,
    -2.3982285245075998e-05,
    2.0904234952920368e-06,
    -3.7230763047369276e-07,
    -1.0585705549674146e-08,
    -5.8138798302825403e-11,
    2.7080049362631943e-13,
    -6.9244749406392e-18,
]
CELL = 1.0 / 4096.0
STEP = 0.1
PENALTY = 3.0
BF = jnp.bfloat16
F32 = jnp.float32
MESH = pl.DeviceIdType.MESH
CYCLE = ((0, 0), (0, 1), (1, 1), (1, 0))
AXES = ("gx", "gy", "gz")

PCOL, PCOLT, RM, RK, RMT, LM, LMT, LK = range(8)


def rounded(table):
    return table.astype(np.float32).astype(ml_dtypes.bfloat16).astype(np.float64)


def best_scale(table):
    tried = 1.0 + np.arange(2048) / 2048.0
    wrong = [np.square(rounded(table * t) / t - table).sum() for t in tried]
    return tried[int(np.argmin(wrong))]


def make_tables():
    magic = np.zeros((16, 16))
    kinetic = np.zeros((16, 16))
    for r in range(16):
        for c in range(16):
            if -8 <= c - r <= 7:
                magic[r, c] = MAGIC[c - r + 8]
            if abs(c - r) <= 14:
                kinetic[r, c] = KINETIC[abs(c - r)]
    new = np.arange(256)
    py, pz, yy, zz = new // 128, new // 64 % 2, new // 8 % 8, new % 8
    old = (8 * py + yy) * 16 + 8 * pz + zz
    pcol = np.zeros((256, 256))
    pcol[old, new] = 1.0
    eye = np.eye(16)
    rm = np.kron(magic, magic).T[old][:, old]
    rk = -0.5 * (np.kron(kinetic, eye) + np.kron(eye, kinetic))[old][:, old]
    lm = np.kron(magic, eye)
    lk = -0.5 * np.kron(kinetic, eye)
    row = slice(7, 8)
    left = best_scale(magic[row])
    right = best_scale(np.kron(magic[row], magic[row]))
    curve = best_scale(np.concatenate([kinetic[row], 2.0 * kinetic[row]]))
    out = [pcol, pcol.T, rm * right, rk * curve, rm.T * right]
    out += [lm * left, lm.T * left, lk * curve]
    stack = np.stack(out).astype(np.float32).astype(ml_dtypes.bfloat16)
    return stack, float((left * right) ** -2), float(1.0 / curve)


def plan():
    first, messages, slot_of = 4, [], [0] * 4
    for dx in (-1, 0, 1):
        for dy in (-1, 0, 1):
            if dx == dy == 0:
                continue
            ex, ey = -dx, -dy
            px, py = (0 if ex < 0 else 1), (0 if ey < 0 else 1)
            count = (1 if ex else 2) * (1 if ey else 2)
            if ex and ey:
                index = CYCLE.index((px, py))
            elif ex:
                index = 2 * px
            else:
                index = 1 if py else 3
            messages.append(((ex, ey, 0), index, first, count))
            slot_of += [len(messages)] * count
            first += count
    return messages, slot_of


def mm(a, b):
    return jnp.dot(a, b, preferred_element_type=F32)


def mm_nt(a, b):
    return lax.dot_general(a, b, (((1,), (1,)), ((), ())), preferred_element_type=F32)


def iota(shape, dim):
    return lax.broadcasted_iota(jnp.int32, shape, dim)


def to_octants(value):
    rows = []
    for px in range(2):
        for block in range(4):
            rows.append(
                jnp.concatenate(
                    [
                        value[px * 128 + x * 16 : px * 128 + x * 16 + 16, block * 64 : block * 64 + 64]
                        for x in range(8)
                    ],
                    axis=1,
                )
            )
    return jnp.concatenate(rows, axis=0)


def from_octants(value):
    rows = []
    for px in range(2):
        for x in range(8):
            rows.append(
                jnp.concatenate(
                    [
                        value[(px * 4 + block) * 16 : (px * 4 + block) * 16 + 16, x * 64 : x * 64 + 64]
                        for block in range(4)
                    ],
                    axis=1,
                )
            )
    return jnp.concatenate(rows, axis=0)


def kernel(
    counts, messages, scale_v, scale_k,
    box_hbm, anchor_ref, pot_hbm, tables_hbm, same_hbm,
    out_ref,
    box_ref, pot_ref, tab, same, ex1, ex2, recv1, recv2,
    turned, halo, halo_x, hx, hy, hz, hxy, hxz, hyz, hxyz,
    load_sem, send_sem, recv_sem, pass_send, pass_recv, halo_send, halo_recv,
):
    me = [lax.axis_index(name) for name in AXES]

    def device(offset):
        return tuple(
            lax.rem(me[i] + (offset[i] + counts[i]), counts[i]) if offset[i] else me[i]
            for i in range(3)
        )

    ups = (1,) if counts[2] == 2 else (-1, 1)
    low = ups[0]
    reach = {m[0] for m in messages} | {(0, 0, up) for up in ups}
    reach |= {(-1, 0, low), (0, -1, low), (-1, -1, low)}
    reach |= {(1, 0, -low), (0, 1, -low), (1, 1, -low)}
    reach = sorted({(x, y, abs(z) if counts[2] == 2 else z) for x, y, z in reach})
    barrier = pltpu.get_barrier_semaphore()
    for offset in reach:
        pl.semaphore_signal(barrier, inc=1, device_id=device(offset), device_id_type=MESH)

    loads = [
        pltpu.make_async_copy(src, dst, load_sem.at[n])
        for n, (src, dst) in enumerate(
            [
                (pot_hbm, pot_ref),
                (box_hbm, box_ref),
                (tables_hbm.at[pl.ds(0, 2)], tab.at[pl.ds(0, 2)]),
                (tables_hbm.at[pl.ds(2, 6)], tab.at[pl.ds(2, 6)]),
                (same_hbm, same),
            ]
        )
    ]
    for load in loads:
        load.start()

    row_f = iota((16, 128), 0)
    lane_f = iota((16, 128), 1) % 16
    coord = []
    for i in range(3):
        along = anchor_ref[0, 0, i].astype(F32)
        square = jnp.where(iota((16, 16), 0) == iota((16, 16), 1), along, 0.0)
        coord.append(jnp.sum(square, axis=1, keepdims=True).astype(jnp.int32))
    touch = functools.reduce(
        jnp.maximum,
        [((c == 0) | (c == REGION - 1)).astype(F32) for c in coord],
    )
    rank = jnp.sum(jnp.where(row_f < lane_f, touch, 0.0), axis=0, keepdims=True)
    touched = jnp.sum(jnp.where(row_f == lane_f, touch, 0.0), axis=0, keepdims=True)
    row_s = iota((80, 128), 0)
    lane_s = iota((80, 128), 1)
    slab = row_s // 16
    octant = jnp.where(slab == 4, 0, jnp.where(slab == 2, 3, jnp.where(slab == 3, 2, slab)))
    octant = octant * 2 + row_s // 8 % 2
    select = jnp.where(
        (octant == lane_s // 16) & ((row_s % 8).astype(F32) == rank) & (touched > 0.5), 1.0, 0.0
    ).astype(BF)
    lanes = iota((16, 128), 1)
    hots = []
    for p in range(8):
        hot, first = None, 0
        for i, bit in enumerate((p // 4, p // 2 % 2, p % 2)):
            span = REGION * counts[i]
            value = coord[i] + (me[i] * REGION + bit)
            value = jnp.where(value >= span, value - span, value) + first
            part = (lanes == value).astype(F32)
            hot = part if hot is None else hot + part
            first += span
        hots.append(hot)
    hot = jnp.concatenate(hots, axis=0).astype(BF)

    loads[0].wait()
    z = iota((40, 384), 0)
    lane = iota((40, 384), 1)
    base = lane - ((z // 8) * 64 + z % 8)
    own = None
    for y in range(8):
        picked = jnp.concatenate(
            [pot_ref[pl.ds(by * 8 + y, 40, stride=40), :] for by in range(5)], axis=0
        ).astype(BF)
        part = mm(picked, (base == 8 * y).astype(F32).astype(BF))
        own = part if own is None else own + part
    for by in range(5):
        halo[by] = jnp.concatenate(
            [own[by * 40 : by * 40 + 40], jnp.zeros((8, 384), F32)], axis=0
        ).astype(BF)

    halo_x[...] = jnp.concatenate(
        [own[by * 40 : by * 40 + 8] for by in range(5)] + [jnp.zeros((8, 384), F32)], axis=0
    ).astype(BF)
    pl.semaphore_wait(barrier, len(reach))
    def remote(src, dst, send, recv, offset):
        return pltpu.make_async_remote_copy(
            src_ref=src, dst_ref=dst, send_sem=send, recv_sem=recv,
            device_id=device(offset), device_id_type=MESH,
        )

    halos = [
        remote(src, dst, halo_send.at[n], halo_recv.at[n], offset)
        for n, (src, dst, offset) in enumerate(
            [
                (halo_x, hx, (-1, 0, 0)),
                (halo.at[pl.ds(0, 1)], hy, (0, -1, 0)),
                (halo.at[:, :, pl.ds(0, 128)], hz, (0, 0, low)),
                (halo_x.at[pl.ds(0, 16)], hxy, (-1, -1, 0)),
                (halo_x.at[:, pl.ds(0, 128)], hxz, (-1, 0, low)),
                (halo.at[pl.ds(0, 1), :, pl.ds(0, 128)], hyz, (0, -1, low)),
                (halo_x.at[pl.ds(0, 16), pl.ds(0, 128)], hxyz, (-1, -1, low)),
            ]
        )
    ]
    for copy in halos:
        copy.start()

    loads[1].wait()
    loads[2].wait()
    permuted = mm(box_ref[...], tab[PCOL])
    halves = []
    for half in range(2):
        turned[half] = permuted[:, half * 128 : half * 128 + 128]
        halves.append(
            jnp.concatenate([turned[half, pl.ds(x, 16, stride=16), :] for x in range(16)], axis=0)
        )
    current_f = jnp.concatenate(halves, axis=1)

    def spread(sweep, source, target):
        for offset, index, first, count in messages:
            remote(
                source.at[pl.ds(index, count)], target.at[0, pl.ds(first, count)],
                send_sem.at[sweep], recv_sem.at[sweep], offset,
            ).start()
        landed = target.at[0, pl.ds(4, 12)]
        copies = [remote(landed, landed, send_sem.at[sweep], recv_sem.at[sweep], (1, 0, 0))]
        own = [
            remote(
                source.at[pl.ds(0, 4)], target.at[2 * n, pl.ds(0, 4)],
                pass_send.at[sweep, 0, n], pass_recv.at[sweep, 0, n], (0, 0, -up if counts[2] > 2 else up),
            )
            for n, up in enumerate(ups)
        ]
        for copy in own:
            copy.start()
        return copies, own

    def pass_on(sweep, target):
        copies = [
            remote(
                target.at[0, pl.ds(4, 12)], target.at[1 + n, pl.ds(4, 12)],
                pass_send.at[sweep, 1, n], pass_recv.at[sweep, 1, n], (0, 0, -up if counts[2] > 2 else up),
            )
            for n, up in enumerate(ups)
        ]
        for copy in copies:
            copy.start()
        return copies

    def export(sweep, octs):
        if sweep == 0:
            listed = mm(select, jnp.concatenate([octs, hot], axis=1))
            ex1[...] = listed.astype(BF).reshape(5, 16, 640)
            return spread(0, ex1, recv1)
        ex2[...] = mm(select, octs).astype(BF).reshape(5, 16, 512)
        return spread(1, ex2, recv2)

    current = current_f.astype(BF)
    octs_f = to_octants(current_f)
    octs = octs_f.astype(BF)
    copies, owns = export(0, octs)

    mask_own = mm_nt(hot, hot) > 2.5
    same_own = (iota((128, 128), 0) % 16 == iota((128, 128), 1) % 16).astype(F32).astype(BF)
    delta = jnp.where(row_f == lane_f, PENALTY, 0.0)
    sent = list(halos)

    def weights(overlap, mask, table, extra):
        width = overlap.shape[1]
        kept = jnp.where(mask, overlap, 0.0).reshape(8, 16, width).sum(axis=0)
        high = kept.astype(BF).astype(F32)
        both = mm(jnp.concatenate([high, kept - high], axis=0).astype(BF), table)
        coupling = (both[:16] + both[16:]) * CELL
        if extra is not None:
            coupling = coupling + extra
        copied = jnp.concatenate([coupling] * 8, axis=0)
        return jnp.where(mask, copied, 0.0).astype(BF)

    masks = []
    potential = None
    for sweep in range(SWEEPS):
        if sweep:
            copies, owns = export(sweep, octs)
            current = from_octants(octs_f).astype(BF)
        target = recv1 if sweep == 0 else recv2

        if sweep == 0:
            loads[3].wait()
        on_grid = mm(tab[LM], mm(current, tab[RM]).astype(BF))
        kinetic = (mm(current, tab[RK]) + mm(tab[LK], current)) * scale_k

        if sweep == 0:
            for copy in halos:
                copy.wait_recv()
            pieces = []
            hx_f, hxz_f = hx[...].astype(F32), hxz[...].astype(F32)
            for by in range(6):
                if by < 5:
                    a, c = halo[by].astype(F32), hz[by].astype(F32)
                    b, d = hx_f[by * 8 : by * 8 + 8], hxz_f[by * 8 : by * 8 + 8]
                else:
                    a, c = hy[0].astype(F32), hyz[0].astype(F32)
                    b, d = hxy[...].astype(F32)[:8], hxyz[...].astype(F32)[:8]
                body = jnp.concatenate([a[:40], b], axis=0)
                side = jnp.concatenate([c[:40], d], axis=0)
                pieces.append(
                    jnp.concatenate(
                        [body[:, :256], jnp.concatenate([body[:, 256:320], side[:, :64]], axis=1)], axis=1
                    )
                )
            pieces.append(jnp.zeros((96, 384), F32))
            extended = jnp.concatenate(pieces, axis=0).astype(BF)
            column = iota((16, 384), 1)
            blocks = []
            depth = jnp.concatenate([coord[2]] * 16, axis=0)
            for py in range(2):
                start = (coord[1] + py) * 48 + coord[0] * 8
                rows = jnp.concatenate(
                    [(column == start + x).astype(F32) for x in range(16)], axis=0
                ).astype(BF)
                taken = mm(rows, extended)
                block = taken[:, :128]
                for bz in range(1, 5):
                    block = jnp.where(depth == bz, taken[:, bz * 64 : bz * 64 + 128], block)
                blocks.append(block * scale_v)
                if py == 0:
                    for copy in copies:
                        copy.wait_recv()
                    passed = pass_on(sweep, target)
            potential = jnp.concatenate(blocks, axis=1)

        weighted = (potential * on_grid).astype(BF)
        applied = mm(tab[LMT], mm(weighted, tab[RMT]).astype(BF)) + kinetic

        if sweep == 0:
            for copy in owns + passed:
                copy.wait_recv()
            loads[4].wait()
        applied = to_octants(applied)
        mixed = (applied - PENALTY * octs_f).astype(BF)
        w_own = weights(mm_nt(mixed, octs), mask_own, same_own, delta)
        correction = mm(w_own, octs)
        if sweep:
            for copy in sent:
                copy.wait_send()
            for copy in copies:
                copy.wait_recv()
            passed = pass_on(sweep, target)
            for copy in owns:
                copy.wait_recv()
        for group in range(1 + len(ups)):
            if group == 1 and sweep:
                for copy in copies + owns + passed:
                    copy.wait_send()
                for copy in passed:
                    copy.wait_recv()
            skip = 4 if group == 1 else 0
            received = target[group, skip:].reshape(256 - skip * 16, target.shape[3])
            if sweep == 0:
                masks.append(mm_nt(hot, received[:, 512:]) > 2.5)
            received = received[:, :512]
            w_near = weights(mm_nt(mixed, received), masks[group], same[skip * 16 :, skip * 16 :], None)
            correction = correction + mm(w_near, received)
        if sweep == 0:
            sent += copies + owns + passed
        octs = (octs_f - STEP * (applied - correction)).astype(BF)
        octs_f = octs.astype(F32)

    back = mm(from_octants(octs_f).astype(BF), tab[PCOLT])
    for half in range(2):
        for x in range(16):
            turned[half, pl.ds(x, 16, stride=16), :] = back[
                x * 16 : x * 16 + 16, half * 128 : half * 128 + 128
            ]
    out_ref[...] = jnp.concatenate([turned[0], turned[1]], axis=1).astype(BF)


def solution(mesh):
    counts = tuple(mesh.shape[name] for name in AXES)
    messages, slot_of = plan()
    slot = np.repeat(np.array(slot_of), 16)
    item = np.arange(256) % 8
    same = (slot[:, None] == slot[None, :]) & (item[:, None] == item[None, :])
    same = same.astype(np.float32).astype(ml_dtypes.bfloat16)
    tables, scale_v, scale_k = make_tables()
    layers = 2 if counts[2] == 2 else 3
    vmem = pl.BlockSpec(memory_space=pltpu.VMEM)
    anyspace = pl.BlockSpec(memory_space=pl.ANY)

    def local(boxes, anchors, potential):
        shape = boxes.shape
        out = pl.pallas_call(
            functools.partial(kernel, counts, messages, scale_v, scale_k),
            out_shape=jax.ShapeDtypeStruct((256, 256), BF),
            in_specs=[anyspace, vmem, anyspace, anyspace, anyspace],
            out_specs=vmem,
            scratch_shapes=[
                pltpu.VMEM((256, 256), BF),
                pltpu.VMEM((1600, 40), F32),
                pltpu.VMEM(tables.shape, BF),
                pltpu.VMEM(same.shape, BF),
                pltpu.VMEM((5, 16, 640), BF),
                pltpu.VMEM((5, 16, 512), BF),
                pltpu.VMEM((layers, 16, 16, 640), BF),
                pltpu.VMEM((layers, 16, 16, 512), BF),
                pltpu.VMEM((2, 256, 128), F32),
                pltpu.VMEM((5, 48, 384), BF),
                pltpu.VMEM((48, 384), BF),
                pltpu.VMEM((48, 384), BF),
                pltpu.VMEM((1, 48, 384), BF),
                pltpu.VMEM((5, 48, 128), BF),
                pltpu.VMEM((16, 384), BF),
                pltpu.VMEM((48, 128), BF),
                pltpu.VMEM((1, 48, 128), BF),
                pltpu.VMEM((16, 128), BF),
                pltpu.SemaphoreType.DMA((5,)),
                pltpu.SemaphoreType.DMA((SWEEPS,)),
                pltpu.SemaphoreType.DMA((SWEEPS,)),
                pltpu.SemaphoreType.DMA((SWEEPS, 2, 2)),
                pltpu.SemaphoreType.DMA((SWEEPS, 2, 2)),
                pltpu.SemaphoreType.DMA((7,)),
                pltpu.SemaphoreType.DMA((7,)),
            ],
            compiler_params=pltpu.CompilerParams(
                collective_id=0, has_side_effects=True, vmem_limit_bytes=55040 * 1024
            ),
        )(
            boxes.reshape(256, 256),
            jnp.transpose(anchors, (0, 1, 4, 2, 3)),
            potential.reshape(1600, 40),
            jnp.asarray(tables),
            jnp.asarray(same),
        )
        return out.reshape(shape)

    placed = (
        P("gx", "gy", "gz", None, None, None),
        P("gx", "gy", "gz", None, None),
        P("gx", "gy", "gz"),
    )
    return jax.shard_map(
        local,
        mesh=mesh,
        in_specs=placed,
        out_specs=P("gx", "gy", "gz", None, None, None),
        check_vma=False,
    )
```

```python
import functools

import jax
import jax.numpy as jnp
import ml_dtypes
import numpy as np
from jax import lax
from jax.experimental import pallas as pl
from jax.experimental.pallas import tpu as pltpu
from jax.sharding import PartitionSpec as P

REGION = 5
SWEEPS = 2
MAGIC = [
    8.433424733352934e-07,
    -1.290557201342061e-05,
    8.76298447621056e-05,
    -0.00030158038132690465,
    0.001747237136729939,
    -0.009420470302010804,
    0.023738214637249424,
    0.0612625895831208,
    0.9940415697834004,
    -0.06048952891969835,
    -0.021030251609303816,
    0.013372634148547948,
    -0.0034412814449349387,
    0.0004944322768868992,
    -5.185986881173433e-05,
    2.7273449291197967e-06,
]
KINETIC = [
    -3.55369228991319,
    2.2191465938911166,
    -0.6156141465570069,
    0.2371780582153806,
    -0.0822663999742123,
    0.0220702918848226,
    -0.004097656893426338,
    0.00045167920287502236,
    -2.3982285245075998e-05,
    2.0904234952920368e-06,
    -3.7230763047369276e-07,
    -1.0585705549674146e-08,
    -5.8138798302825403e-11,
    2.7080049362631943e-13,
    -6.9244749406392e-18,
]
CELL = 1.0 / 4096.0
STEP = 0.1
PENALTY = 3.0
BF = jnp.bfloat16
F32 = jnp.float32
MESH = pl.DeviceIdType.MESH
CYCLE = ((0, 0), (0, 1), (1, 1), (1, 0))
AXES = ("gx", "gy", "gz")

PCOL, PCOLT, RM, RK, RMT, LM, LMT, LK = range(8)


def rounded(table):
    return table.astype(np.float32).astype(ml_dtypes.bfloat16).astype(np.float64)


def best_scale(table):
    tried = 1.0 + np.arange(2048) / 2048.0
    wrong = [np.square(rounded(table * t) / t - table).sum() for t in tried]
    return tried[int(np.argmin(wrong))]


def make_tables():
    magic = np.zeros((16, 16))
    kinetic = np.zeros((16, 16))
    for r in range(16):
        for c in range(16):
            if -8 <= c - r <= 7:
                magic[r, c] = MAGIC[c - r + 8]
            if abs(c - r) <= 14:
                kinetic[r, c] = KINETIC[abs(c - r)]
    new = np.arange(256)
    py, pz, yy, zz = new // 128, new // 64 % 2, new // 8 % 8, new % 8
    old = (8 * py + yy) * 16 + 8 * pz + zz
    pcol = np.zeros((256, 256))
    pcol[old, new] = 1.0
    eye = np.eye(16)
    rm = np.kron(magic, magic).T[old][:, old]
    rk = -0.5 * (np.kron(kinetic, eye) + np.kron(eye, kinetic))[old][:, old]
    lm = np.kron(magic, eye)
    lk = -0.5 * np.kron(kinetic, eye)
    row = slice(7, 8)
    left = best_scale(magic[row])
    right = best_scale(np.kron(magic[row], magic[row]))
    curve = best_scale(np.concatenate([kinetic[row], 2.0 * kinetic[row]]))
    out = [pcol, pcol.T, rm * right, rk * curve, rm.T * right]
    out += [lm * left, lm.T * left, lk * curve]
    stack = np.stack(out).astype(np.float32).astype(ml_dtypes.bfloat16)
    return stack, float((left * right) ** -2), float(1.0 / curve)


def plan():
    first, messages, slot_of = 4, [], [0] * 4
    for dx in (-1, 0, 1):
        for dy in (-1, 0, 1):
            if dx == dy == 0:
                continue
            ex, ey = -dx, -dy
            px, py = (0 if ex < 0 else 1), (0 if ey < 0 else 1)
            count = (1 if ex else 2) * (1 if ey else 2)
            if ex and ey:
                index = CYCLE.index((px, py))
            elif ex:
                index = 2 * px
            else:
                index = 1 if py else 3
            messages.append(((ex, ey, 0), index, first, count))
            slot_of += [len(messages)] * count
            first += count
    messages.sort(key=lambda m: (m[0][0] * m[0][1] == 0, m[0][1] == 0))
    return messages, slot_of


def mm(a, b):
    return jnp.dot(a, b, preferred_element_type=F32)


def mm_nt(a, b):
    return lax.dot_general(a, b, (((1,), (1,)), ((), ())), preferred_element_type=F32)


def iota(shape, dim):
    return lax.broadcasted_iota(jnp.int32, shape, dim)


def to_octants(value):
    rows = []
    for px in range(2):
        for block in range(4):
            rows.append(
                jnp.concatenate(
                    [
                        value[px * 128 + x * 16 : px * 128 + x * 16 + 16, block * 64 : block * 64 + 64]
                        for x in range(8)
                    ],
                    axis=1,
                )
            )
    return jnp.concatenate(rows, axis=0)


def from_octants(value):
    rows = []
    for px in range(2):
        for x in range(8):
            rows.append(
                jnp.concatenate(
                    [
                        value[(px * 4 + block) * 16 : (px * 4 + block) * 16 + 16, x * 64 : x * 64 + 64]
                        for block in range(4)
                    ],
                    axis=1,
                )
            )
    return jnp.concatenate(rows, axis=0)


def kernel(
    counts, messages, scale_v, scale_k,
    box_hbm, anchor_ref, pot_hbm, tables_hbm, same_hbm,
    out_ref,
    box_ref, pot_ref, tab, same, ex1, ex2, recv1, recv2,
    turned, halo, halo_x, hx, hy, hz, hxy, hxz, hyz, hxyz,
    load_sem, send_sem, recv_sem, pass_send, pass_recv, halo_send, halo_recv,
):
    me = [lax.axis_index(name) for name in AXES]

    def device(offset):
        return tuple(
            lax.rem(me[i] + (offset[i] + counts[i]), counts[i]) if offset[i] else me[i]
            for i in range(3)
        )

    ups = (1,) if counts[2] == 2 else (-1, 1)
    low = ups[0]
    reach = {m[0] for m in messages} | {(0, 0, up) for up in ups}
    reach |= {(-1, 0, low), (0, -1, low), (-1, -1, low)}
    reach |= {(1, 0, -low), (0, 1, -low), (1, 1, -low)}
    reach = sorted({(x, y, abs(z) if counts[2] == 2 else z) for x, y, z in reach})
    barrier = pltpu.get_barrier_semaphore()
    for offset in reach:
        pl.semaphore_signal(barrier, inc=1, device_id=device(offset), device_id_type=MESH)

    loads = [
        pltpu.make_async_copy(src, dst, load_sem.at[n])
        for n, (src, dst) in enumerate(
            [
                (pot_hbm, pot_ref),
                (box_hbm, box_ref),
                (tables_hbm.at[pl.ds(0, 2)], tab.at[pl.ds(0, 2)]),
                (tables_hbm.at[pl.ds(2, 6)], tab.at[pl.ds(2, 6)]),
                (same_hbm, same),
            ]
        )
    ]
    for load in loads:
        load.start()

    row_f = iota((16, 128), 0)
    lane_f = iota((16, 128), 1) % 16
    coord = []
    for i in range(3):
        along = anchor_ref[0, 0, i].astype(F32)
        square = jnp.where(iota((16, 16), 0) == iota((16, 16), 1), along, 0.0)
        coord.append(jnp.sum(square, axis=1, keepdims=True).astype(jnp.int32))
    touch = functools.reduce(
        jnp.maximum,
        [((c == 0) | (c == REGION - 1)).astype(F32) for c in coord],
    )
    rank = jnp.sum(jnp.where(row_f < lane_f, touch, 0.0), axis=0, keepdims=True)
    touched = jnp.sum(jnp.where(row_f == lane_f, touch, 0.0), axis=0, keepdims=True)
    row_s = iota((80, 128), 0)
    lane_s = iota((80, 128), 1)
    slab = row_s // 16
    octant = jnp.where(slab == 4, 0, jnp.where(slab == 2, 3, jnp.where(slab == 3, 2, slab)))
    octant = octant * 2 + row_s // 8 % 2
    select = jnp.where(
        (octant == lane_s // 16) & ((row_s % 8).astype(F32) == rank) & (touched > 0.5), 1.0, 0.0
    ).astype(BF)
    lanes = iota((16, 128), 1)
    hots = []
    for p in range(8):
        hot, first = None, 0
        for i, bit in enumerate((p // 4, p // 2 % 2, p % 2)):
            span = REGION * counts[i]
            value = coord[i] + (me[i] * REGION + bit)
            value = jnp.where(value >= span, value - span, value) + first
            part = (lanes == value).astype(F32)
            hot = part if hot is None else hot + part
            first += span
        hots.append(hot)
    hot = jnp.concatenate(hots, axis=0).astype(BF)

    loads[0].wait()
    z = iota((40, 384), 0)
    lane = iota((40, 384), 1)
    base = lane - ((z // 8) * 64 + z % 8)
    own = None
    for y in range(8):
        picked = jnp.concatenate(
            [pot_ref[pl.ds(by * 8 + y, 40, stride=40), :] for by in range(5)], axis=0
        ).astype(BF)
        part = mm(picked, (base == 8 * y).astype(F32).astype(BF))
        own = part if own is None else own + part
    for by in range(5):
        halo[by] = jnp.concatenate(
            [own[by * 40 : by * 40 + 40], jnp.zeros((8, 384), F32)], axis=0
        ).astype(BF)

    halo_x[...] = jnp.concatenate(
        [own[by * 40 : by * 40 + 8] for by in range(5)] + [jnp.zeros((8, 384), F32)], axis=0
    ).astype(BF)
    pl.semaphore_wait(barrier, len(reach))
    def remote(src, dst, send, recv, offset):
        return pltpu.make_async_remote_copy(
            src_ref=src, dst_ref=dst, send_sem=send, recv_sem=recv,
            device_id=device(offset), device_id_type=MESH,
        )

    halos = [
        remote(src, dst, halo_send.at[n], halo_recv.at[n], offset)
        for n, (src, dst, offset) in enumerate(
            [
                (halo_x, hx, (-1, 0, 0)),
                (halo.at[pl.ds(0, 1)], hy, (0, -1, 0)),
                (halo.at[:, :, pl.ds(0, 128)], hz, (0, 0, low)),
                (halo_x.at[pl.ds(0, 16)], hxy, (-1, -1, 0)),
                (halo_x.at[:, pl.ds(0, 128)], hxz, (-1, 0, low)),
                (halo.at[pl.ds(0, 1), :, pl.ds(0, 128)], hyz, (0, -1, low)),
                (halo_x.at[pl.ds(0, 16), pl.ds(0, 128)], hxyz, (-1, -1, low)),
            ]
        )
    ]
    for copy in halos:
        copy.start()

    loads[1].wait()
    loads[2].wait()
    permuted = mm(box_ref[...], tab[PCOL])
    halves = []
    for half in range(2):
        turned[half] = permuted[:, half * 128 : half * 128 + 128]
        halves.append(
            jnp.concatenate([turned[half, pl.ds(x, 16, stride=16), :] for x in range(16)], axis=0)
        )
    current_f = jnp.concatenate(halves, axis=1)

    def spread(sweep, source, target):
        for offset, index, first, count in messages:
            remote(
                source.at[pl.ds(index, count)], target.at[0, pl.ds(first, count)],
                send_sem.at[sweep], recv_sem.at[sweep], offset,
            ).start()
        landed = target.at[0, pl.ds(4, 12)]
        copies = [remote(landed, landed, send_sem.at[sweep], recv_sem.at[sweep], (1, 0, 0))]
        own = [
            remote(
                source.at[pl.ds(0, 4)], target.at[2 * n, pl.ds(0, 4)],
                pass_send.at[sweep, 0, n], pass_recv.at[sweep, 0, n], (0, 0, -up if counts[2] > 2 else up),
            )
            for n, up in enumerate(ups)
        ]
        for copy in own:
            copy.start()
        return copies, own

    def pass_on(sweep, target):
        copies = [
            remote(
                target.at[0, pl.ds(4, 12)], target.at[1 + n, pl.ds(4, 12)],
                pass_send.at[sweep, 1, n], pass_recv.at[sweep, 1, n], (0, 0, -up if counts[2] > 2 else up),
            )
            for n, up in enumerate(ups)
        ]
        for copy in copies:
            copy.start()
        return copies

    def export(sweep, octs):
        if sweep == 0:
            listed = mm(select, jnp.concatenate([octs, hot], axis=1))
            ex1[...] = listed.astype(BF).reshape(5, 16, 640)
            return spread(0, ex1, recv1)
        ex2[...] = mm(select, octs).astype(BF).reshape(5, 16, 512)
        return spread(1, ex2, recv2)

    current = current_f.astype(BF)
    octs_f = to_octants(current_f)
    octs = octs_f.astype(BF)
    copies, owns = export(0, octs)

    mask_own = mm_nt(hot, hot) > 2.5
    same_own = (iota((128, 128), 0) % 16 == iota((128, 128), 1) % 16).astype(F32).astype(BF)
    delta = jnp.where(row_f == lane_f, PENALTY, 0.0)
    sent = list(halos)

    def weights(overlap, mask, table, extra):
        width = overlap.shape[1]
        kept = jnp.where(mask, overlap, 0.0).reshape(8, 16, width).sum(axis=0)
        high = kept.astype(BF).astype(F32)
        both = mm(jnp.concatenate([high, kept - high], axis=0).astype(BF), table)
        coupling = (both[:16] + both[16:]) * CELL
        if extra is not None:
            coupling = coupling + extra
        copied = jnp.concatenate([coupling] * 8, axis=0)
        return jnp.where(mask, copied, 0.0).astype(BF)

    masks = []
    potential = None
    for sweep in range(SWEEPS):
        if sweep:
            copies, owns = export(sweep, octs)
            current = from_octants(octs_f).astype(BF)
        target = recv1 if sweep == 0 else recv2

        if sweep == 0:
            loads[3].wait()
        on_grid = mm(tab[LM], mm(current, tab[RM]).astype(BF))
        kinetic = (mm(current, tab[RK]) + mm(tab[LK], current)) * scale_k

        if sweep == 0:
            for copy in halos:
                copy.wait_recv()
            pieces = []
            hx_f, hxz_f = hx[...].astype(F32), hxz[...].astype(F32)
            for by in range(6):
                if by < 5:
                    a, c = halo[by].astype(F32), hz[by].astype(F32)
                    b, d = hx_f[by * 8 : by * 8 + 8], hxz_f[by * 8 : by * 8 + 8]
                else:
                    a, c = hy[0].astype(F32), hyz[0].astype(F32)
                    b, d = hxy[...].astype(F32)[:8], hxyz[...].astype(F32)[:8]
                body = jnp.concatenate([a[:40], b], axis=0)
                side = jnp.concatenate([c[:40], d], axis=0)
                pieces.append(
                    jnp.concatenate(
                        [body[:, :256], jnp.concatenate([body[:, 256:320], side[:, :64]], axis=1)], axis=1
                    )
                )
            pieces.append(jnp.zeros((96, 384), F32))
            extended = jnp.concatenate(pieces, axis=0).astype(BF)
            column = iota((16, 384), 1)
            blocks = []
            depth = jnp.concatenate([coord[2]] * 16, axis=0)
            for py in range(2):
                start = (coord[1] + py) * 48 + coord[0] * 8
                rows = jnp.concatenate(
                    [(column == start + x).astype(F32) for x in range(16)], axis=0
                ).astype(BF)
                taken = mm(rows, extended)
                block = taken[:, :128]
                for bz in range(1, 5):
                    block = jnp.where(depth == bz, taken[:, bz * 64 : bz * 64 + 128], block)
                blocks.append(block * scale_v)
            potential = jnp.concatenate(blocks, axis=1)

        if sweep == 0:
            for copy in copies:
                copy.wait_recv()
            passed = pass_on(sweep, target)
        weighted = (potential * on_grid).astype(BF)
        applied = mm(tab[LMT], mm(weighted, tab[RMT]).astype(BF)) + kinetic

        if sweep == 0:
            for copy in owns:
                copy.wait_recv()
            loads[4].wait()
        applied = to_octants(applied)
        mixed = (applied - PENALTY * octs_f).astype(BF)
        w_own = weights(mm_nt(mixed, octs), mask_own, same_own, delta)
        correction = mm(w_own, octs)
        if sweep:
            for copy in sent:
                copy.wait_send()
            for copy in copies:
                copy.wait_recv()
            passed = pass_on(sweep, target)
            for copy in owns:
                copy.wait_recv()
        for group in range(1 + len(ups)):
            if group == 1:
                if sweep:
                    for copy in copies + owns + passed:
                        copy.wait_send()
                for copy in passed:
                    copy.wait_recv()
            skip = 4 if group == 1 else 0
            received = target[group, skip:].reshape(256 - skip * 16, target.shape[3])
            if sweep == 0:
                masks.append(mm_nt(hot, received[:, 512:]) > 2.5)
            received = received[:, :512]
            w_near = weights(mm_nt(mixed, received), masks[group], same[skip * 16 :, skip * 16 :], None)
            correction = correction + mm(w_near, received)
        if sweep == 0:
            sent += copies + owns + passed
        octs = (octs_f - STEP * (applied - correction)).astype(BF)
        octs_f = octs.astype(F32)

    back = mm(from_octants(octs_f).astype(BF), tab[PCOLT])
    for half in range(2):
        for x in range(16):
            turned[half, pl.ds(x, 16, stride=16), :] = back[
                x * 16 : x * 16 + 16, half * 128 : half * 128 + 128
            ]
    out_ref[...] = jnp.concatenate([turned[0], turned[1]], axis=1).astype(BF)


def solution(mesh):
    counts = tuple(mesh.shape[name] for name in AXES)
    messages, slot_of = plan()
    slot = np.repeat(np.array(slot_of), 16)
    item = np.arange(256) % 8
    same = (slot[:, None] == slot[None, :]) & (item[:, None] == item[None, :])
    same = same.astype(np.float32).astype(ml_dtypes.bfloat16)
    tables, scale_v, scale_k = make_tables()
    layers = 2 if counts[2] == 2 else 3
    vmem = pl.BlockSpec(memory_space=pltpu.VMEM)
    anyspace = pl.BlockSpec(memory_space=pl.ANY)

    def local(boxes, anchors, potential):
        shape = boxes.shape
        out = pl.pallas_call(
            functools.partial(kernel, counts, messages, scale_v, scale_k),
            out_shape=jax.ShapeDtypeStruct((256, 256), BF),
            in_specs=[anyspace, vmem, anyspace, anyspace, anyspace],
            out_specs=vmem,
            scratch_shapes=[
                pltpu.VMEM((256, 256), BF),
                pltpu.VMEM((1600, 40), F32),
                pltpu.VMEM(tables.shape, BF),
                pltpu.VMEM(same.shape, BF),
                pltpu.VMEM((5, 16, 640), BF),
                pltpu.VMEM((5, 16, 512), BF),
                pltpu.VMEM((layers, 16, 16, 640), BF),
                pltpu.VMEM((layers, 16, 16, 512), BF),
                pltpu.VMEM((2, 256, 128), F32),
                pltpu.VMEM((5, 48, 384), BF),
                pltpu.VMEM((48, 384), BF),
                pltpu.VMEM((48, 384), BF),
                pltpu.VMEM((1, 48, 384), BF),
                pltpu.VMEM((5, 48, 128), BF),
                pltpu.VMEM((16, 384), BF),
                pltpu.VMEM((48, 128), BF),
                pltpu.VMEM((1, 48, 128), BF),
                pltpu.VMEM((16, 128), BF),
                pltpu.SemaphoreType.DMA((5,)),
                pltpu.SemaphoreType.DMA((SWEEPS,)),
                pltpu.SemaphoreType.DMA((SWEEPS,)),
                pltpu.SemaphoreType.DMA((SWEEPS, 2, 2)),
                pltpu.SemaphoreType.DMA((SWEEPS, 2, 2)),
                pltpu.SemaphoreType.DMA((7,)),
                pltpu.SemaphoreType.DMA((7,)),
            ],
            compiler_params=pltpu.CompilerParams(
                collective_id=0, has_side_effects=True, vmem_limit_bytes=55040 * 1024
            ),
        )(
            boxes.reshape(256, 256),
            jnp.transpose(anchors, (0, 1, 4, 2, 3)),
            potential.reshape(1600, 40),
            jnp.asarray(tables),
            jnp.asarray(same),
        )
        return out.reshape(shape)

    placed = (
        P("gx", "gy", "gz", None, None, None),
        P("gx", "gy", "gz", None, None),
        P("gx", "gy", "gz"),
    )
    return jax.shard_map(
        local,
        mesh=mesh,
        in_specs=placed,
        out_specs=P("gx", "gy", "gz", None, None, None),
        check_vma=False,
    )
```

```python
import functools

import jax
import jax.numpy as jnp
import ml_dtypes
import numpy as np
from jax import lax
from jax.experimental import pallas as pl
from jax.experimental.pallas import tpu as pltpu
from jax.sharding import PartitionSpec as P

REGION = 5
SWEEPS = 2
MAGIC = [
    8.433424733352934e-07,
    -1.290557201342061e-05,
    8.76298447621056e-05,
    -0.00030158038132690465,
    0.001747237136729939,
    -0.009420470302010804,
    0.023738214637249424,
    0.0612625895831208,
    0.9940415697834004,
    -0.06048952891969835,
    -0.021030251609303816,
    0.013372634148547948,
    -0.0034412814449349387,
    0.0004944322768868992,
    -5.185986881173433e-05,
    2.7273449291197967e-06,
]
KINETIC = [
    -3.55369228991319,
    2.2191465938911166,
    -0.6156141465570069,
    0.2371780582153806,
    -0.0822663999742123,
    0.0220702918848226,
    -0.004097656893426338,
    0.00045167920287502236,
    -2.3982285245075998e-05,
    2.0904234952920368e-06,
    -3.7230763047369276e-07,
    -1.0585705549674146e-08,
    -5.8138798302825403e-11,
    2.7080049362631943e-13,
    -6.9244749406392e-18,
]
CELL = 1.0 / 4096.0
STEP = 0.1
PENALTY = 3.0
BF = jnp.bfloat16
F32 = jnp.float32
MESH = pl.DeviceIdType.MESH
CYCLE = ((0, 0), (0, 1), (1, 1), (1, 0))
AXES = ("gx", "gy", "gz")

PCOL, PCOLT, RM, RK, RMT, LM, LMT, LK = range(8)


def rounded(table):
    return table.astype(np.float32).astype(ml_dtypes.bfloat16).astype(np.float64)


def best_scale(table):
    tried = 1.0 + np.arange(2048) / 2048.0
    wrong = [np.square(rounded(table * t) / t - table).sum() for t in tried]
    return tried[int(np.argmin(wrong))]


def make_tables():
    magic = np.zeros((16, 16))
    kinetic = np.zeros((16, 16))
    for r in range(16):
        for c in range(16):
            if -8 <= c - r <= 7:
                magic[r, c] = MAGIC[c - r + 8]
            if abs(c - r) <= 14:
                kinetic[r, c] = KINETIC[abs(c - r)]
    new = np.arange(256)
    py, pz, yy, zz = new // 128, new // 64 % 2, new // 8 % 8, new % 8
    old = (8 * py + yy) * 16 + 8 * pz + zz
    pcol = np.zeros((256, 256))
    pcol[old, new] = 1.0
    eye = np.eye(16)
    rm = np.kron(magic, magic).T[old][:, old]
    rk = -0.5 * (np.kron(kinetic, eye) + np.kron(eye, kinetic))[old][:, old]
    lm = np.kron(magic, eye)
    lk = -0.5 * np.kron(kinetic, eye)
    row = slice(7, 8)
    left = best_scale(magic[row])
    right = best_scale(np.kron(magic[row], magic[row]))
    curve = best_scale(np.concatenate([kinetic[row], 2.0 * kinetic[row]]))
    out = [pcol, pcol.T, rm * right, rk * curve, rm.T * right]
    out += [lm * left, lm.T * left, lk * curve]
    stack = np.stack(out).astype(np.float32).astype(ml_dtypes.bfloat16)
    return stack, float((left * right) ** -2), float(1.0 / curve)


def plan():
    first, messages, slot_of = 4, [], [0] * 4
    for dx in (-1, 0, 1):
        for dy in (-1, 0, 1):
            if dx == dy == 0:
                continue
            ex, ey = -dx, -dy
            px, py = (0 if ex < 0 else 1), (0 if ey < 0 else 1)
            count = (1 if ex else 2) * (1 if ey else 2)
            if ex and ey:
                index = CYCLE.index((px, py))
            elif ex:
                index = 2 * px
            else:
                index = 1 if py else 3
            messages.append(((ex, ey, 0), index, first, count))
            slot_of += [len(messages)] * count
            first += count
    messages.sort(key=lambda m: (m[0][0] * m[0][1] == 0, m[0][1] == 0))
    return messages, slot_of


def mm(a, b):
    return jnp.dot(a, b, preferred_element_type=F32)


def mm_nt(a, b):
    return lax.dot_general(a, b, (((1,), (1,)), ((), ())), preferred_element_type=F32)


def iota(shape, dim):
    return lax.broadcasted_iota(jnp.int32, shape, dim)


def to_octants(value):
    rows = []
    for px in range(2):
        for block in range(4):
            rows.append(
                jnp.concatenate(
                    [
                        value[px * 128 + x * 16 : px * 128 + x * 16 + 16, block * 64 : block * 64 + 64]
                        for x in range(8)
                    ],
                    axis=1,
                )
            )
    return jnp.concatenate(rows, axis=0)


def from_octants(value):
    rows = []
    for px in range(2):
        for x in range(8):
            rows.append(
                jnp.concatenate(
                    [
                        value[(px * 4 + block) * 16 : (px * 4 + block) * 16 + 16, x * 64 : x * 64 + 64]
                        for block in range(4)
                    ],
                    axis=1,
                )
            )
    return jnp.concatenate(rows, axis=0)


def kernel(
    counts, messages, scale_v, scale_k,
    box_hbm, anchor_ref, pot_hbm, tables_hbm, same_hbm,
    out_ref,
    box_ref, pot_ref, tab, same, ex1, ex2, recv1, recv2,
    turned, halo, halo_x, hx, hy, hz, hxy, hxz, hyz, hxyz,
    load_sem, send_sem, recv_sem, pass_send, pass_recv, halo_send, halo_recv,
):
    me = [lax.axis_index(name) for name in AXES]

    def device(offset):
        return tuple(
            lax.rem(me[i] + (offset[i] + counts[i]), counts[i]) if offset[i] else me[i]
            for i in range(3)
        )

    ups = (1,) if counts[2] == 2 else (-1, 1)
    low = ups[0]
    reach = {m[0] for m in messages} | {(0, 0, up) for up in ups}
    reach |= {(-1, 0, low), (0, -1, low), (-1, -1, low)}
    reach |= {(1, 0, -low), (0, 1, -low), (1, 1, -low)}
    reach = sorted({(x, y, abs(z) if counts[2] == 2 else z) for x, y, z in reach})
    barrier = pltpu.get_barrier_semaphore()
    for offset in reach:
        pl.semaphore_signal(barrier, inc=1, device_id=device(offset), device_id_type=MESH)

    loads = [
        pltpu.make_async_copy(src, dst, load_sem.at[n])
        for n, (src, dst) in enumerate(
            [
                (pot_hbm, pot_ref),
                (box_hbm, box_ref),
                (tables_hbm.at[pl.ds(0, 2)], tab.at[pl.ds(0, 2)]),
                (tables_hbm.at[pl.ds(2, 6)], tab.at[pl.ds(2, 6)]),
                (same_hbm, same),
            ]
        )
    ]
    for load in loads:
        load.start()

    row_f = iota((16, 128), 0)
    lane_f = iota((16, 128), 1) % 16
    coord = []
    for i in range(3):
        along = anchor_ref[0, 0, i].astype(F32)
        square = jnp.where(iota((16, 16), 0) == iota((16, 16), 1), along, 0.0)
        coord.append(jnp.sum(square, axis=1, keepdims=True).astype(jnp.int32))
    touch = functools.reduce(
        jnp.maximum,
        [((c == 0) | (c == REGION - 1)).astype(F32) for c in coord],
    )
    rank = jnp.sum(jnp.where(row_f < lane_f, touch, 0.0), axis=0, keepdims=True)
    touched = jnp.sum(jnp.where(row_f == lane_f, touch, 0.0), axis=0, keepdims=True)
    row_s = iota((80, 128), 0)
    lane_s = iota((80, 128), 1)
    slab = row_s // 16
    octant = jnp.where(slab == 4, 0, jnp.where(slab == 2, 3, jnp.where(slab == 3, 2, slab)))
    octant = octant * 2 + row_s // 8 % 2
    select = jnp.where(
        (octant == lane_s // 16) & ((row_s % 8).astype(F32) == rank) & (touched > 0.5), 1.0, 0.0
    ).astype(BF)
    lanes = iota((16, 128), 1)
    hots = []
    for p in range(8):
        hot, first = None, 0
        for i, bit in enumerate((p // 4, p // 2 % 2, p % 2)):
            span = REGION * counts[i]
            value = coord[i] + (me[i] * REGION + bit)
            value = jnp.where(value >= span, value - span, value) + first
            part = (lanes == value).astype(F32)
            hot = part if hot is None else hot + part
            first += span
        hots.append(hot)
    hot = jnp.concatenate(hots, axis=0).astype(BF)

    loads[0].wait()
    z = iota((40, 384), 0)
    lane = iota((40, 384), 1)
    base = lane - ((z // 8) * 64 + z % 8)
    own = None
    for y in range(8):
        picked = jnp.concatenate(
            [pot_ref[pl.ds(by * 8 + y, 40, stride=40), :] for by in range(5)], axis=0
        ).astype(BF)
        part = mm(picked, (base == 8 * y).astype(F32).astype(BF))
        own = part if own is None else own + part
    for by in range(5):
        halo[by] = jnp.concatenate(
            [own[by * 40 : by * 40 + 40], jnp.zeros((8, 384), F32)], axis=0
        ).astype(BF)

    halo_x[...] = jnp.concatenate(
        [own[by * 40 : by * 40 + 8] for by in range(5)] + [jnp.zeros((8, 384), F32)], axis=0
    ).astype(BF)
    pl.semaphore_wait(barrier, len(reach))
    def remote(src, dst, send, recv, offset):
        return pltpu.make_async_remote_copy(
            src_ref=src, dst_ref=dst, send_sem=send, recv_sem=recv,
            device_id=device(offset), device_id_type=MESH,
        )

    halos = [
        remote(src, dst, halo_send.at[n], halo_recv.at[n], offset)
        for n, (src, dst, offset) in enumerate(
            [
                (halo_x.at[pl.ds(0, 16)], hxy, (-1, -1, 0)),
                (halo_x.at[pl.ds(0, 16), pl.ds(0, 128)], hxyz, (-1, -1, low)),
                (halo.at[pl.ds(0, 1)], hy, (0, -1, 0)),
                (halo.at[pl.ds(0, 1), :, pl.ds(0, 128)], hyz, (0, -1, low)),
                (halo_x, hx, (-1, 0, 0)),
                (halo_x.at[:, pl.ds(0, 128)], hxz, (-1, 0, low)),
                (halo.at[:, :, pl.ds(0, 128)], hz, (0, 0, low)),
            ]
        )
    ]
    for copy in halos:
        copy.start()

    loads[1].wait()
    loads[2].wait()
    permuted = mm(box_ref[...], tab[PCOL])
    halves = []
    for half in range(2):
        turned[half] = permuted[:, half * 128 : half * 128 + 128]
        halves.append(
            jnp.concatenate([turned[half, pl.ds(x, 16, stride=16), :] for x in range(16)], axis=0)
        )
    current_f = jnp.concatenate(halves, axis=1)

    def spread(sweep, source, target):
        for offset, index, first, count in messages:
            remote(
                source.at[pl.ds(index, count)], target.at[0, pl.ds(first, count)],
                send_sem.at[sweep], recv_sem.at[sweep], offset,
            ).start()
        landed = target.at[0, pl.ds(4, 12)]
        copies = [remote(landed, landed, send_sem.at[sweep], recv_sem.at[sweep], (1, 0, 0))]
        own = [
            remote(
                source.at[pl.ds(0, 4)], target.at[2 * n, pl.ds(0, 4)],
                pass_send.at[sweep, 0, n], pass_recv.at[sweep, 0, n], (0, 0, -up if counts[2] > 2 else up),
            )
            for n, up in enumerate(ups)
        ]
        for copy in own:
            copy.start()
        return copies, own

    def pass_on(sweep, target):
        copies = [
            remote(
                target.at[0, pl.ds(4, 12)], target.at[1 + n, pl.ds(4, 12)],
                pass_send.at[sweep, 1, n], pass_recv.at[sweep, 1, n], (0, 0, -up if counts[2] > 2 else up),
            )
            for n, up in enumerate(ups)
        ]
        for copy in copies:
            copy.start()
        return copies

    def export(sweep, octs):
        if sweep == 0:
            listed = mm(select, jnp.concatenate([octs, hot], axis=1))
            ex1[...] = listed.astype(BF).reshape(5, 16, 640)
            return spread(0, ex1, recv1)
        ex2[...] = mm(select, octs).astype(BF).reshape(5, 16, 512)
        return spread(1, ex2, recv2)

    current = current_f.astype(BF)
    octs_f = to_octants(current_f)
    octs = octs_f.astype(BF)
    copies, owns = export(0, octs)

    mask_own = mm_nt(hot, hot) > 2.5
    same_own = (iota((128, 128), 0) % 16 == iota((128, 128), 1) % 16).astype(F32).astype(BF)
    delta = jnp.where(row_f == lane_f, PENALTY, 0.0)
    sent = list(halos)

    def weights(overlap, mask, table, extra):
        width = overlap.shape[1]
        kept = jnp.where(mask, overlap, 0.0).reshape(8, 16, width).sum(axis=0)
        high = kept.astype(BF).astype(F32)
        both = mm(jnp.concatenate([high, kept - high], axis=0).astype(BF), table)
        coupling = (both[:16] + both[16:]) * CELL
        if extra is not None:
            coupling = coupling + extra
        copied = jnp.concatenate([coupling] * 8, axis=0)
        return jnp.where(mask, copied, 0.0).astype(BF)

    masks = []
    potential = None
    for sweep in range(SWEEPS):
        if sweep:
            copies, owns = export(sweep, octs)
            current = from_octants(octs_f).astype(BF)
        target = recv1 if sweep == 0 else recv2

        if sweep == 0:
            loads[3].wait()
        on_grid = mm(tab[LM], mm(current, tab[RM]).astype(BF))
        kinetic = (mm(current, tab[RK]) + mm(tab[LK], current)) * scale_k

        if sweep == 0:
            for copy in halos:
                copy.wait_recv()
            pieces = []
            hx_f, hxz_f = hx[...].astype(F32), hxz[...].astype(F32)
            for by in range(6):
                if by < 5:
                    a, c = halo[by].astype(F32), hz[by].astype(F32)
                    b, d = hx_f[by * 8 : by * 8 + 8], hxz_f[by * 8 : by * 8 + 8]
                else:
                    a, c = hy[0].astype(F32), hyz[0].astype(F32)
                    b, d = hxy[...].astype(F32)[:8], hxyz[...].astype(F32)[:8]
                body = jnp.concatenate([a[:40], b], axis=0)
                side = jnp.concatenate([c[:40], d], axis=0)
                pieces.append(
                    jnp.concatenate(
                        [body[:, :256], jnp.concatenate([body[:, 256:320], side[:, :64]], axis=1)], axis=1
                    )
                )
            pieces.append(jnp.zeros((96, 384), F32))
            extended = jnp.concatenate(pieces, axis=0).astype(BF)
            column = iota((16, 384), 1)
            blocks = []
            depth = jnp.concatenate([coord[2]] * 16, axis=0)
            for py in range(2):
                start = (coord[1] + py) * 48 + coord[0] * 8
                rows = jnp.concatenate(
                    [(column == start + x).astype(F32) for x in range(16)], axis=0
                ).astype(BF)
                taken = mm(rows, extended)
                block = taken[:, :128]
                for bz in range(1, 5):
                    block = jnp.where(depth == bz, taken[:, bz * 64 : bz * 64 + 128], block)
                blocks.append(block * scale_v)
            potential = jnp.concatenate(blocks, axis=1)

        if sweep == 0:
            for copy in copies:
                copy.wait_recv()
            passed = pass_on(sweep, target)
        weighted = (potential * on_grid).astype(BF)
        applied = mm(tab[LMT], mm(weighted, tab[RMT]).astype(BF)) + kinetic

        if sweep == 0:
            for copy in owns:
                copy.wait_recv()
            loads[4].wait()
        applied = to_octants(applied)
        mixed = (applied - PENALTY * octs_f).astype(BF)
        w_own = weights(mm_nt(mixed, octs), mask_own, same_own, delta)
        correction = mm(w_own, octs)
        if sweep:
            for copy in sent:
                copy.wait_send()
            for copy in copies:
                copy.wait_recv()
            passed = pass_on(sweep, target)
            for copy in owns:
                copy.wait_recv()
        for group in range(1 + len(ups)):
            if group == 1:
                if sweep:
                    for copy in copies + owns + passed:
                        copy.wait_send()
                for copy in passed:
                    copy.wait_recv()
            skip = 4 if group == 1 else 0
            received = target[group, skip:].reshape(256 - skip * 16, target.shape[3])
            if sweep == 0:
                masks.append(mm_nt(hot, received[:, 512:]) > 2.5)
            received = received[:, :512]
            w_near = weights(mm_nt(mixed, received), masks[group], same[skip * 16 :, skip * 16 :], None)
            correction = correction + mm(w_near, received)
        if sweep == 0:
            sent += copies + owns + passed
        octs = (octs_f - STEP * (applied - correction)).astype(BF)
        octs_f = octs.astype(F32)

    back = mm(from_octants(octs_f).astype(BF), tab[PCOLT])
    for half in range(2):
        for x in range(16):
            turned[half, pl.ds(x, 16, stride=16), :] = back[
                x * 16 : x * 16 + 16, half * 128 : half * 128 + 128
            ]
    out_ref[...] = jnp.concatenate([turned[0], turned[1]], axis=1).astype(BF)


def solution(mesh):
    counts = tuple(mesh.shape[name] for name in AXES)
    messages, slot_of = plan()
    slot = np.repeat(np.array(slot_of), 16)
    item = np.arange(256) % 8
    same = (slot[:, None] == slot[None, :]) & (item[:, None] == item[None, :])
    same = same.astype(np.float32).astype(ml_dtypes.bfloat16)
    tables, scale_v, scale_k = make_tables()
    layers = 2 if counts[2] == 2 else 3
    vmem = pl.BlockSpec(memory_space=pltpu.VMEM)
    anyspace = pl.BlockSpec(memory_space=pl.ANY)

    def local(boxes, anchors, potential):
        shape = boxes.shape
        out = pl.pallas_call(
            functools.partial(kernel, counts, messages, scale_v, scale_k),
            out_shape=jax.ShapeDtypeStruct((256, 256), BF),
            in_specs=[anyspace, vmem, anyspace, anyspace, anyspace],
            out_specs=vmem,
            scratch_shapes=[
                pltpu.VMEM((256, 256), BF),
                pltpu.VMEM((1600, 40), F32),
                pltpu.VMEM(tables.shape, BF),
                pltpu.VMEM(same.shape, BF),
                pltpu.VMEM((5, 16, 640), BF),
                pltpu.VMEM((5, 16, 512), BF),
                pltpu.VMEM((layers, 16, 16, 640), BF),
                pltpu.VMEM((layers, 16, 16, 512), BF),
                pltpu.VMEM((2, 256, 128), F32),
                pltpu.VMEM((5, 48, 384), BF),
                pltpu.VMEM((48, 384), BF),
                pltpu.VMEM((48, 384), BF),
                pltpu.VMEM((1, 48, 384), BF),
                pltpu.VMEM((5, 48, 128), BF),
                pltpu.VMEM((16, 384), BF),
                pltpu.VMEM((48, 128), BF),
                pltpu.VMEM((1, 48, 128), BF),
                pltpu.VMEM((16, 128), BF),
                pltpu.SemaphoreType.DMA((5,)),
                pltpu.SemaphoreType.DMA((SWEEPS,)),
                pltpu.SemaphoreType.DMA((SWEEPS,)),
                pltpu.SemaphoreType.DMA((SWEEPS, 2, 2)),
                pltpu.SemaphoreType.DMA((SWEEPS, 2, 2)),
                pltpu.SemaphoreType.DMA((7,)),
                pltpu.SemaphoreType.DMA((7,)),
            ],
            compiler_params=pltpu.CompilerParams(
                collective_id=0, has_side_effects=True, vmem_limit_bytes=55040 * 1024
            ),
        )(
            boxes.reshape(256, 256),
            jnp.transpose(anchors, (0, 1, 4, 2, 3)),
            potential.reshape(1600, 40),
            jnp.asarray(tables),
            jnp.asarray(same),
        )
        return out.reshape(shape)

    placed = (
        P("gx", "gy", "gz", None, None, None),
        P("gx", "gy", "gz", None, None),
        P("gx", "gy", "gz"),
    )
    return jax.shard_map(
        local,
        mesh=mesh,
        in_specs=placed,
        out_specs=P("gx", "gy", "gz", None, None, None),
        check_vma=False,
    )
```
